512 devices in a mesh: scen: 8 (over x, core), reach: 64 (over y, z).
Axes of the slice: x: 4, y: 8, z: 8, core: 2. Of those that a mesh axis runs over, the one named last changes fastest.
Arguments:
- perturb: float32 [8, 2, 1048576], P('scen', None, 'reach'), may hold values from -4 to 4
- resist: float32 [1048576], P('reach'), may hold values from 0.01 to 0.06
- flow_rate: float32 [8], P('scen'), may hold values from 3 to 5
- head_plan: float32 [8, 16], P('scen'), may hold values from -2 to 2
- valve_plan: float32 [8, 16], P('scen'), may hold values from 0.2 to 5
Outputs:
- basis_rows: float32 [2, 1048576, 128], P(None, ('reach', 'scen'))
- triangle: float32 [128, 128], replicated
The draws below stay inside these ranges and needn't reach their ends.
All inputs are finite; a program needn't handle non-finite values.
Results may differ from the reference program's by a relative error of at most 0.0009.
The reference program's roundings to bfloat16 on the way (of `columns`) count: a program that leaves them out, or rounds other values in their place, can miss the bound.
Values may be sent and summed in bfloat16 or wider, within the bound.
No kernel may reach another device: no remote copies, remote signals or barrier semaphores. Data moves between devices by JAX's collectives and lax.ppermute only.
A program may use at most 64 MiB of HBM per device.

```python
import math
import jax
import jax.numpy as jnp
from jax import lax

STEPS = 16
SCENARIOS = 8
CELLS = 1048576
COLS = 128


def block_levels(own_key, shape, shards, least, largest):
    level = 1.0
    for dim, blocks in shards:
        steps = jax.random.uniform(jax.random.fold_in(jax.random.fold_in(own_key, 6), dim), (blocks,), jnp.float32, least / len(shards), largest / len(shards))
        level = level * jnp.repeat(jnp.exp(steps), shape[dim] // blocks).reshape((-1,) + (1,) * (len(shape) - 1 - dim))
    return level


def bell_draw(stream_key, extent, scale, bound, split=(), held_as=jnp.bfloat16):
    loudness = block_levels(stream_key, extent, split, -0.22, 0.18) if split else 1.0
    array = jax.random.normal(stream_key, extent, jnp.float32) * scale * loudness
    return jnp.minimum(jnp.maximum(array, -bound), bound).astype(held_as)


def setup_inputs(seed: int = 0) -> dict:
    keys = jax.random.split(jax.random.key(seed), 6)
    return {
        "perturb": bell_draw(keys[0], (SCENARIOS, 2, CELLS), 1.0, 4.0, ((0, 8), (2, 64)), jnp.float32),
        "resist": jnp.clip(jnp.exp(math.log(0.06) - 1.7917595 * jax.random.uniform(keys[1], (CELLS,), jnp.float32) ** block_levels(keys[1], (CELLS,), ((0, 64),), -0.2, 0.2)), 0.01, 0.06),
        "flow_rate": jnp.clip(3.0 + 2.0 * jax.random.uniform(keys[2], (SCENARIOS,), jnp.float32) ** block_levels(keys[2], (SCENARIOS,), ((0, 8),), -0.2, 0.2), 3.0, 5.0),
        "head_plan": jnp.clip(jax.random.uniform(keys[3], (SCENARIOS, STEPS), jnp.float32, -2.0, 2.0) * block_levels(keys[3], (SCENARIOS, STEPS), ((0, 8),), -0.4, 0.0), -2.0, 2.0),
        "valve_plan": jnp.clip(jnp.exp(math.log(5.0) - 3.218876 * jax.random.uniform(keys[4], (SCENARIOS, STEPS), jnp.float32) ** block_levels(keys[4], (SCENARIOS, STEPS), ((0, 8),), -0.2, 0.2)), 0.2, 5.0),
    }


SHARES = (0.06, 0.04, 0.025, 0.015)
RETAINS = (0.2, 0.5, 0.8, 0.95)

def carried(head_now, flow_now, states, resist):
    friction = resist * flow_now * jnp.abs(flow_now) + (states[0] + states[1] + states[2] + states[3])
    return (head_now + flow_now - friction, head_now - flow_now + friction)

def update(current_flow, states, from_left, from_right, left_mask, right_mask, head_left, opening):
    new_head = 0.5 * (from_left + from_right)
    new_flow = 0.5 * (from_left - from_right)
    orifice = 1.0 / (1.0 + opening)
    new_head = jnp.where(left_mask, head_left, new_head)
    new_flow = jnp.where(left_mask, head_left - from_right, new_flow)
    new_head = jnp.where(right_mask, from_left * orifice, new_head)
    new_flow = jnp.where(right_mask, opening * from_left * orifice, new_flow)
    change = new_flow - current_flow
    new_states = tuple((RETAINS[which] * states[which] + SHARES[which] * change for which in range(4)))
    return (new_head, new_flow, new_states)

def reference(perturb, resist, flow_rate, head_plan, valve_plan):
    position = jnp.arange(CELLS)
    left_mask = position == 0
    right_mask = position == CELLS - 1
    nothing = jnp.zeros((1,), jnp.float32)
    pieces = []
    for member in range(SCENARIOS):
        steady = flow_rate[member]
        running = jnp.cumsum(resist * (steady * jnp.abs(steady) / CELLS))
        head_now = head_plan[member, 0] - running + perturb[member, 0]
        flow_now = steady * CELLS ** (-0.5) + perturb[member, 1]
        states = tuple((jnp.zeros((CELLS,), jnp.float32) for which in range(4)))
        frames = []
        for moment in range(STEPS):
            forward, backward = carried(head_now, flow_now, states, resist)
            from_left = jnp.concatenate([nothing, forward[:-1]])
            from_right = jnp.concatenate([backward[1:], nothing])
            head_now, flow_now, states = update(flow_now, states, from_left, from_right, left_mask, right_mask, head_plan[member, moment], valve_plan[member, moment])
            frames.append(jnp.stack([head_now, flow_now]).astype(jnp.bfloat16))
        pieces.append(jnp.stack(frames))
    columns = jnp.concatenate(pieces, axis=0)
    widened = columns.astype(jnp.float32)
    moments = jnp.einsum('cfr,dfr->cd', widened, widened, precision=lax.Precision.HIGHEST) / (2 * CELLS)
    factor_low = jnp.linalg.cholesky(moments)
    inverse = lax.linalg.triangular_solve(factor_low, jnp.eye(COLS, dtype=jnp.float32), left_side=True, lower=True)
    basis_rows = jnp.einsum('cfr,dc->frd', widened, inverse, precision=lax.Precision.HIGHEST)
    return (basis_rows, factor_low.T)
```

```python
import jax
import jax.numpy as jnp
from jax import lax
from jax.experimental import pallas as pl
from jax.experimental.pallas import tpu as pltpu
from jax.sharding import PartitionSpec as P

STEPS = 16
SHARES = (0.06, 0.04, 0.025, 0.015)
RETAINS = (0.2, 0.5, 0.8, 0.95)
LANES = 128
HALO = 16
SCENS = 8
REACHES = 64
COLS = SCENS * STEPS
CELLS = 1048576
PART = CELLS // REACHES
SHARE = PART // SCENS
BLOCKS = SHARE // LANES
RIGHT_ROW = 2 * BLOCKS
LEFT_ROW = RIGHT_ROW + 2
HEAD_ROW = LEFT_ROW + 2
VALVE_ROW = HEAD_ROW + 1
FLOW_ROW = VALVE_ROW + 1
WINDOW = 40
WIDE = BLOCKS + 2
PANEL = 32
CHUNK = 512
EXACT = lax.Precision.HIGHEST


def params():
    return pltpu.CompilerParams(vmem_limit_bytes=40 * 1024 * 1024)


def edges_kernel(state_ref, resist_ref, out_ref):
    lane = lax.broadcasted_iota(jnp.int32, (1, LANES), 1)
    last = 2 * PART // LANES - 2

    def ends(first, final):
        return jnp.where(lane < HALO, first, jnp.where(lane >= LANES - HALO, final, 0.0))

    resist = resist_ref[...]
    total = jnp.sum(jnp.sum(resist, axis=0, keepdims=True), axis=1, keepdims=True)
    row = jnp.concatenate(
        [
            ends(state_ref[0:1, :], state_ref[last : last + 1, :]),
            ends(state_ref[1:2, :], state_ref[last + 1 : last + 2, :]),
            ends(resist[0:1, :], resist[LANES - 1 : LANES, :]),
            jnp.broadcast_to(total, (1, LANES)),
        ],
        axis=0,
    )
    out_ref[...] = jnp.broadcast_to(row[None], (REACHES, 4, LANES))


def window_kernel(state_ref, resist_ref, edge_ref, flow_ref, head_ref, valve_ref, out_ref, aux_ref):
    reach = lax.axis_index("reach")
    scen = lax.axis_index("scen")
    left = edge_ref[jnp.maximum(reach - 1, 0)]
    right = edge_ref[jnp.minimum(reach + 1, REACHES - 1)]
    rows = 2 * BLOCKS
    for which in range(SCENS):
        start = which * rows
        out_ref[which, 0:rows, :] = state_ref[start : start + rows, :]
        if which < SCENS - 1:
            out_ref[which, RIGHT_ROW : RIGHT_ROW + 2, :] = state_ref[start + rows : start + rows + 2, :]
        else:
            out_ref[which, RIGHT_ROW : RIGHT_ROW + 2, :] = right[0:2]
        if which > 0:
            out_ref[which, LEFT_ROW : LEFT_ROW + 2, :] = state_ref[start - 2 : start, :]
        else:
            out_ref[which, LEFT_ROW : LEFT_ROW + 2, :] = left[0:2]
        out_ref[which, HEAD_ROW:WINDOW, :] = jnp.zeros((WINDOW - HEAD_ROW, LANES), jnp.float32)
        out_ref[which, HEAD_ROW : HEAD_ROW + 1, 0:STEPS] = head_ref[...]
        out_ref[which, VALVE_ROW : VALVE_ROW + 1, 0:STEPS] = valve_ref[...]
        out_ref[which, FLOW_ROW : FLOW_ROW + 1, :] = jnp.full((1, LANES), flow_ref[0], jnp.float32)

    first = scen * BLOCKS
    inner_left = resist_ref[pl.ds(jnp.maximum(first - 1, 0), 1), :]
    inner_right = resist_ref[pl.ds(jnp.minimum(first + BLOCKS, LANES - 1), 1), :]
    row_left = jnp.where(scen == 0, left[2:3], inner_left)
    row_right = jnp.where(scen == SCENS - 1, right[2:3], inner_right)
    mine = resist_ref[pl.ds(pl.multiple_of(first, BLOCKS), BLOCKS), :]
    spread = jnp.concatenate([mine, row_right, row_left, jnp.zeros((6, LANES), jnp.float32)], axis=0)
    place = lax.broadcasted_iota(jnp.int32, (REACHES, 1), 0)
    upstream = jnp.sum(jnp.where(place < reach, edge_ref[:, 3, :], 0.0), axis=0, keepdims=True)
    row_id = lax.broadcasted_iota(jnp.int32, (LANES, 1), 0)
    before = jnp.sum(jnp.where(row_id < first, resist_ref[...], 0.0), axis=0, keepdims=True)
    base = upstream + jnp.sum(before, axis=1, keepdims=True)
    a = lax.broadcasted_iota(jnp.int32, (LANES, LANES), 0)
    b = lax.broadcasted_iota(jnp.int32, (LANES, LANES), 1)
    upto = jnp.where(a <= b, 1.0, 0.0).astype(jnp.float32)
    inside = jnp.dot(spread, upto, precision=EXACT, preferred_element_type=jnp.float32)
    totals = jnp.sum(spread, axis=1, keepdims=True)
    c = lax.broadcasted_iota(jnp.int32, (24, 24), 0)
    d = lax.broadcasted_iota(jnp.int32, (24, 24), 1)
    ahead = jnp.where((d < c) & (c <= BLOCKS) & (d < BLOCKS), 1.0, 0.0)
    ahead = ahead - jnp.where((c == BLOCKS + 1) & (d == BLOCKS + 1), 1.0, 0.0)
    shift = jnp.dot(
        ahead.astype(jnp.float32),
        jnp.broadcast_to(totals, (24, LANES)),
        precision=EXACT,
        preferred_element_type=jnp.float32,
    )
    aux_ref[0:24, :] = spread
    aux_ref[24:48, :] = base + (shift + inside)


def step_kernel(win_ref, aux_ref, cols_ref, gram_ref, wide_ref, plan_ref, kept_ref):
    scen = lax.axis_index("scen")
    reach = lax.axis_index("reach")
    lane = lax.broadcasted_iota(jnp.int32, (SCENS, LANES), 1)
    at_first = (lane == 0) & (scen == 0) & (reach == 0)
    at_last = (lane == LANES - 1) & (scen == SCENS - 1) & (reach == REACHES - 1)
    is_low = lane == 0
    is_high = lane == LANES - 1

    def taken(row):
        return win_ref[pl.ds(row, SCENS, stride=WINDOW), :]

    head_plan = taken(HEAD_ROW)
    valve_plan = taken(VALVE_ROW)
    orifice = 1.0 / (1.0 + valve_plan)
    opened = valve_plan * orifice
    for moment in range(STEPS):
        for which, plan in enumerate((head_plan, orifice, opened)):
            plan_ref[which, moment * SCENS : (moment + 1) * SCENS, :] = jnp.broadcast_to(
                plan[:, moment : moment + 1], (SCENS, LANES)
            )
    steady = taken(FLOW_ROW)
    scale = steady * jnp.abs(steady) * (1.0 / CELLS)
    mean_flow = steady * CELLS ** (-0.5)
    first_head = plan_ref[0, 0:SCENS, :]
    rows = [LEFT_ROW] + [2 * j for j in range(BLOCKS)] + [RIGHT_ROW]
    aux_rows = [BLOCKS + 1] + list(range(BLOCKS)) + [BLOCKS]
    none = jnp.zeros((SCENS, LANES), jnp.float32)
    for j in range(WIDE):
        running = aux_ref[24 + aux_rows[j] : 25 + aux_rows[j], :]
        wide_ref[0, j] = first_head - running * scale + taken(rows[j])
        wide_ref[1, j] = mean_flow + taken(rows[j] + 1)
        for state in range(4):
            wide_ref[2 + state, j] = none
        wide_ref[6, j] = jnp.broadcast_to(aux_ref[aux_rows[j] : aux_rows[j] + 1, :], (SCENS, LANES))

    def one_step(moment, carry):
        plan_rows = pl.ds(pl.multiple_of(moment * SCENS, SCENS), SCENS)
        head_left = plan_ref[0, plan_rows, :]
        small = plan_ref[1, plan_rows, :]
        large = plan_ref[2, plan_rows, :]

        def sent(j):
            head, flow = wide_ref[0, j], wide_ref[1, j]
            friction = wide_ref[6, j] * flow * jnp.abs(flow) + (
                (wide_ref[2, j] + wide_ref[3, j]) + (wide_ref[4, j] + wide_ref[5, j])
            )
            net = flow - friction
            return pltpu.roll(head + net, 1, 1), pltpu.roll(head - net, LANES - 1, 1)

        forward_before, (forward, backward) = None, sent(0)
        for j in range(WIDE):
            forward_after, backward_after = sent(j + 1) if j + 1 < WIDE else (forward, backward)
            if forward_before is None:
                forward_before = forward
            from_left = jnp.where(is_low, forward_before, forward)
            from_right = jnp.where(is_high, backward_after, backward)
            new_head = 0.5 * (from_left + from_right)
            new_flow = 0.5 * (from_left - from_right)
            if j == 1:
                new_head = jnp.where(at_first, head_left, new_head)
                new_flow = jnp.where(at_first, head_left - from_right, new_flow)
            if j == BLOCKS:
                new_head = jnp.where(at_last, from_left * small, new_head)
                new_flow = jnp.where(at_last, from_left * large, new_flow)
            change = new_flow - wide_ref[1, j]
            wide_ref[0, j] = new_head
            wide_ref[1, j] = new_flow
            for state in range(4):
                wide_ref[2 + state, j] = RETAINS[state] * wide_ref[2 + state, j] + SHARES[state] * change
            if 1 <= j <= BLOCKS:
                kept_ref[0, j - 1, plan_rows, :] = new_head
                kept_ref[1, j - 1, plan_rows, :] = new_flow
            forward_before, forward, backward = forward, forward_after, backward_after
        return carry

    lax.fori_loop(0, STEPS, one_step, 0)

    for field in range(2):
        for j in range(BLOCKS):
            for which in range(SCENS):
                piece = kept_ref[field, j, pl.ds(which, STEPS, stride=SCENS), :]
                cols_ref[field, which * STEPS : (which + 1) * STEPS, j * LANES : (j + 1) * LANES] = piece.astype(
                    jnp.bfloat16
                )
    total = None
    for field in range(2):
        columns = cols_ref[field]
        part = lax.dot_general(columns, columns, (((1,), (1,)), ((), ())), preferred_element_type=jnp.float32)
        total = part if total is None else total + part
    gram_ref[...] = total.reshape(SCENS, STEPS, COLS)


def fold_kernel(in_ref, out_ref):
    count, copies = in_ref.shape[0], out_ref.shape[0]
    total = in_ref[0]
    for which in range(1, count):
        total = total + in_ref[which]
    for which in range(copies):
        out_ref[which] = total


def basis_kernel(gram_ref, cols_ref, rows_ref, tri_ref, work_ref, out_ref, sems):
    scale = 1.0 / (2 * CELLS)
    row_id = lax.broadcasted_iota(jnp.int32, (COLS, COLS), 0)
    col_id = lax.broadcasted_iota(jnp.int32, (COLS, COLS), 1)
    work_ref[:, 0:COLS] = gram_ref[...].reshape(COLS, COLS) * scale
    work_ref[:, COLS:] = jnp.where(row_id == col_id, 1.0, 0.0).astype(jnp.float32)
    sub = lax.broadcasted_iota(jnp.int32, (8, 1), 0)
    groups = PANEL // 8
    for panel in range(COLS // PANEL):
        low = panel * PANEL
        left = [work_ref[low + 8 * g : low + 8 * g + 8, 0:COLS] for g in range(groups)]
        right = [work_ref[low + 8 * g : low + 8 * g + 8, COLS:] for g in range(groups)]
        for k in range(PANEL):
            own, inner = divmod(k, 8)
            column = low + k
            row_left = left[own][inner : inner + 1, :]
            row_right = right[own][inner : inner + 1, :]
            inverse = 1.0 / row_left[:, column : column + 1]
            row_left = row_left * inverse
            row_right = row_right * inverse
            for g in range(own, groups):
                factor = left[g][:, column : column + 1]
                if g == own:
                    factor = jnp.where(sub > inner, factor, 0.0)
                left[g] = left[g] - factor * row_left
                right[g] = right[g] - factor * row_right
        for g in range(groups):
            work_ref[low + 8 * g : low + 8 * g + 8, 0:COLS] = left[g]
            work_ref[low + 8 * g : low + 8 * g + 8, COLS:] = right[g]
        if low + PANEL < COLS:
            rows = work_ref[low : low + PANEL, :]
            here = rows[:, 0:COLS]
            own_rows = lax.broadcasted_iota(jnp.int32, (PANEL, COLS), 0) + low
            own_cols = lax.broadcasted_iota(jnp.int32, (PANEL, COLS), 1)
            pivot = jnp.sum(jnp.where(own_rows == own_cols, here, 0.0), axis=1, keepdims=True)
            update = lax.dot_general(
                here / pivot,
                rows,
                (((0,), (0,)), ((), ())),
                precision=EXACT,
                preferred_element_type=jnp.float32,
            )
            work_ref[low + PANEL :, :] = work_ref[low + PANEL :, :] - update[low + PANEL :, :]
    reduced = work_ref[:, 0:COLS]
    pivot = jnp.sum(jnp.where(row_id == col_id, reduced, 0.0), axis=1, keepdims=True)
    root = 1.0 / jnp.sqrt(pivot)
    tri_ref[...] = jnp.where(row_id <= col_id, reduced * root, 0.0)
    inverse = (work_ref[:, COLS:] * root).T
    high = inverse.astype(jnp.bfloat16)
    rest = inverse - high.astype(jnp.float32)
    middle = rest.astype(jnp.bfloat16)
    low_part = (rest - middle.astype(jnp.float32)).astype(jnp.bfloat16)
    copies = []
    for field in range(2):
        for part in range(SHARE // CHUNK):
            piece = cols_ref[field, :, part * CHUNK : (part + 1) * CHUNK].T
            total = jnp.dot(piece, low_part, preferred_element_type=jnp.float32)
            total = total + jnp.dot(piece, middle, preferred_element_type=jnp.float32)
            total = total + jnp.dot(piece, high, preferred_element_type=jnp.float32)
            slot = len(copies)
            out_ref[slot] = total
            copy = pltpu.make_async_copy(
                out_ref.at[slot], rows_ref.at[field, pl.ds(part * CHUNK, CHUNK), :], sems.at[slot]
            )
            copy.start()
            copies.append(copy)
    for copy in copies:
        copy.wait()


def fold(value, copies):
    return pl.pallas_call(
        fold_kernel,
        out_shape=jax.ShapeDtypeStruct((copies,) + value.shape[1:], jnp.float32),
        compiler_params=params(),
    )(value)


def exchanged(value, axis):
    return lax.all_to_all(value, axis, split_axis=0, concat_axis=0, tiled=True)


def local(perturb, resist, flow_rate, head_plan, valve_plan):
    f32 = jnp.float32
    vmem = pl.BlockSpec(memory_space=pltpu.VMEM)
    smem = pl.BlockSpec(memory_space=pltpu.SMEM)
    blocks = PART // LANES
    state = perturb.reshape(2, blocks, LANES).transpose(1, 0, 2).reshape(2 * blocks, LANES)
    resist = resist.reshape(LANES, LANES)
    edges = pl.pallas_call(
        edges_kernel,
        out_shape=jax.ShapeDtypeStruct((REACHES, 4, LANES), f32),
        compiler_params=params(),
    )(state, resist)
    edges = exchanged(edges, "reach")
    windows, aux = pl.pallas_call(
        window_kernel,
        in_specs=[vmem, vmem, vmem, smem, vmem, vmem],
        out_shape=(
            jax.ShapeDtypeStruct((SCENS, WINDOW, LANES), f32),
            jax.ShapeDtypeStruct((48, LANES), f32),
        ),
        compiler_params=params(),
    )(state, resist, edges, flow_rate, head_plan, valve_plan)
    windows = exchanged(windows, "scen").reshape(SCENS * WINDOW, LANES)
    columns, gram = pl.pallas_call(
        step_kernel,
        out_shape=(
            jax.ShapeDtypeStruct((2, COLS, SHARE), jnp.bfloat16),
            jax.ShapeDtypeStruct((SCENS, STEPS, COLS), f32),
        ),
        scratch_shapes=[
            pltpu.VMEM((7, WIDE, SCENS, LANES), f32),
            pltpu.VMEM((3, STEPS * SCENS, LANES), f32),
            pltpu.VMEM((2, BLOCKS, COLS, LANES), f32),
        ],
        compiler_params=params(),
    )(windows, aux)
    gram = fold(exchanged(gram, "scen"), REACHES)
    gram = fold(exchanged(gram, "reach"), SCENS)
    gram = exchanged(gram, "scen")
    chunks = 2 * SHARE // CHUNK
    return pl.pallas_call(
        basis_kernel,
        in_specs=[vmem, vmem],
        out_specs=(pl.BlockSpec(memory_space=pl.ANY), vmem),
        out_shape=(
            jax.ShapeDtypeStruct((2, SHARE, COLS), f32),
            jax.ShapeDtypeStruct((COLS, COLS), f32),
        ),
        scratch_shapes=[
            pltpu.VMEM((COLS, 2 * COLS), f32),
            pltpu.VMEM((chunks, CHUNK, COLS), f32),
            pltpu.SemaphoreType.DMA((chunks,)),
        ],
        compiler_params=params(),
    )(gram, columns)


def solution(mesh):
    in_specs = (P("scen", None, "reach"), P("reach"), P("scen"), P("scen", None), P("scen", None))
    out_specs = (P(None, ("reach", "scen"), None), P())
    return jax.shard_map(local, mesh=mesh, in_specs=in_specs, out_specs=out_specs, check_vma=False)
```

```python
import jax
import jax.numpy as jnp
from jax import lax
from jax.experimental import pallas as pl
from jax.experimental.pallas import tpu as pltpu
from jax.sharding import PartitionSpec as P

STEPS = 16
SHARES = (0.06, 0.04, 0.025, 0.015)
RETAINS = (0.2, 0.5, 0.8, 0.95)
LANES = 128
HALO = 16
SCENS = 8
REACHES = 64
COLS = SCENS * STEPS
CELLS = 1048576
PART = CELLS // REACHES
SHARE = PART // SCENS
BLOCKS = SHARE // LANES
RIGHT_ROW = 2 * BLOCKS
LEFT_ROW = RIGHT_ROW + 2
HEAD_ROW = LEFT_ROW + 2
VALVE_ROW = HEAD_ROW + 1
FLOW_ROW = VALVE_ROW + 1
WINDOW = 40
WIDE = BLOCKS + 2
PANEL = 64
CHUNK = 256
EXACT = lax.Precision.HIGHEST


def params(mib=40):
    return pltpu.CompilerParams(vmem_limit_bytes=mib * 1024 * 1024)


def prepare_kernel(state_hbm, resist_hbm, flow_hbm, head_hbm, valve_hbm, edge_ref, out_ref, state, resist, flow, head, valve, sems):
    loads = []
    for which, (source, target) in enumerate(
        ((resist_hbm, resist), (state_hbm, state), (flow_hbm, flow), (head_hbm, head), (valve_hbm, valve))
    ):
        copy = pltpu.make_async_copy(source, target, sems.at[which])
        copy.start()
        loads.append(copy)
    loads[0].wait()
    lane = lax.broadcasted_iota(jnp.int32, (1, LANES), 1)
    total = jnp.sum(jnp.sum(resist[...], axis=0, keepdims=True), axis=1, keepdims=True)
    ends = jnp.where(
        lane < HALO, resist[0:1, :], jnp.where(lane >= LANES - HALO, resist[LANES - 1 : LANES, :], 0.0)
    )
    upto = ends
    for step in (1, 2, 4, 8):
        upto = upto + jnp.where(lane >= step, pltpu.roll(upto, step, 1), 0.0)
    upto = jnp.where(lane < HALO, upto, upto - upto[:, LANES - 1 : LANES])
    row = jnp.concatenate([ends, upto, jnp.broadcast_to(total, (1, LANES)), ends], axis=0)
    edge_ref[...] = jnp.broadcast_to(row[None], (REACHES, 4, LANES))
    for copy in loads[1:]:
        copy.wait()
    rows = 2 * BLOCKS
    none = jnp.zeros((2, LANES), jnp.float32)
    for which in range(SCENS):
        start = which * rows
        out_ref[which, 0:rows, :] = state[start : start + rows, :]
        after = state[start + rows : start + rows + 2, :] if which < SCENS - 1 else none
        out_ref[which, RIGHT_ROW : RIGHT_ROW + 2, :] = after
        out_ref[which, LEFT_ROW : LEFT_ROW + 2, :] = state[start - 2 : start, :] if which > 0 else none
        out_ref[which, HEAD_ROW:WINDOW, :] = jnp.zeros((WINDOW - HEAD_ROW, LANES), jnp.float32)
        out_ref[which, HEAD_ROW : HEAD_ROW + 1, 0:STEPS] = head[...]
        out_ref[which, VALVE_ROW : VALVE_ROW + 1, 0:STEPS] = valve[...]
        out_ref[which, FLOW_ROW : FLOW_ROW + 1, :] = jnp.full((1, LANES), flow[0], jnp.float32)


def spread_kernel(resist_ref, aux_ref):
    scen = lax.axis_index("scen")
    first = scen * BLOCKS
    row_left = resist_ref[pl.ds(jnp.maximum(first - 1, 0), 1), :]
    row_right = resist_ref[pl.ds(jnp.minimum(first + BLOCKS, LANES - 1), 1), :]
    mine = resist_ref[pl.ds(pl.multiple_of(first, BLOCKS), BLOCKS), :]
    spread = jnp.concatenate([mine, row_right, row_left, jnp.zeros((6, LANES), jnp.float32)], axis=0)
    row_id = lax.broadcasted_iota(jnp.int32, (LANES, 1), 0)
    before = jnp.sum(jnp.where(row_id < first, resist_ref[...], 0.0), axis=0, keepdims=True)
    base = jnp.sum(before, axis=1, keepdims=True)
    a = lax.broadcasted_iota(jnp.int32, (LANES, LANES), 0)
    b = lax.broadcasted_iota(jnp.int32, (LANES, LANES), 1)
    upto = jnp.where(a <= b, 1.0, 0.0).astype(jnp.float32)
    inside = jnp.dot(spread, upto, precision=EXACT, preferred_element_type=jnp.float32)
    totals = jnp.sum(spread, axis=1, keepdims=True)
    c = lax.broadcasted_iota(jnp.int32, (24, 24), 0)
    d = lax.broadcasted_iota(jnp.int32, (24, 24), 1)
    ahead = jnp.where((d < c) & (c <= BLOCKS) & (d < BLOCKS), 1.0, 0.0)
    ahead = ahead - jnp.where((c == BLOCKS + 1) & (d == BLOCKS + 1), 1.0, 0.0)
    shift = jnp.dot(
        ahead.astype(jnp.float32),
        jnp.broadcast_to(totals, (24, LANES)),
        precision=EXACT,
        preferred_element_type=jnp.float32,
    )
    aux_ref[0:24, :] = spread
    aux_ref[24:48, :] = base + (shift + inside)


def outer_kernel(win_ref, out_ref):
    low = lax.axis_index("scen") == 0
    for field in range(2):
        first = win_ref[pl.ds(field, SCENS, stride=WINDOW), :]
        final = win_ref[pl.ds(RIGHT_ROW - 2 + field, SCENS, stride=WINDOW), :]
        out_ref[field * SCENS : (field + 1) * SCENS, :] = jnp.where(low, first, final)


def step_kernel(win_ref, outer_ref, edge_ref, aux_ref, cols_ref, gram_ref, wide_ref, plan_ref, kept_ref):
    scen = lax.axis_index("scen")
    reach = lax.axis_index("reach")
    lane = lax.broadcasted_iota(jnp.int32, (SCENS, LANES), 1)
    at_first = (lane == 0) & (scen == 0) & (reach == 0)
    at_last = (lane == LANES - 1) & (scen == SCENS - 1) & (reach == REACHES - 1)
    is_low = lane == 0
    is_high = lane == LANES - 1

    def taken(row):
        return win_ref[pl.ds(row, SCENS, stride=WINDOW), :]

    head_plan = taken(HEAD_ROW)
    valve_plan = taken(VALVE_ROW)
    orifice = 1.0 / (1.0 + valve_plan)
    opened = valve_plan * orifice
    for moment in range(STEPS):
        for which, plan in enumerate((head_plan, orifice, opened)):
            plan_ref[which, moment * SCENS : (moment + 1) * SCENS, :] = jnp.broadcast_to(
                plan[:, moment : moment + 1], (SCENS, LANES)
            )
    steady = taken(FLOW_ROW)
    scale = steady * jnp.abs(steady) * (1.0 / CELLS)
    mean_flow = steady * CELLS ** (-0.5)
    first_head = plan_ref[0, 0:SCENS, :]
    place = lax.broadcasted_iota(jnp.int32, (REACHES, 1), 0)
    totals = edge_ref[:, 2, :]
    upstream = jnp.sum(jnp.where(place < reach, totals, 0.0), axis=0, keepdims=True)
    through = jnp.sum(jnp.where(place <= reach, totals, 0.0), axis=0, keepdims=True)
    previous = edge_ref[jnp.maximum(reach - 1, 0)]
    following = edge_ref[jnp.minimum(reach + 1, REACHES - 1)]
    none = jnp.zeros((SCENS, LANES), jnp.float32)
    for j in range(WIDE):
        row = [LEFT_ROW, RIGHT_ROW][j > BLOCKS] if j in (0, WIDE - 1) else 2 * (j - 1)
        at = [BLOCKS + 1, BLOCKS][j > BLOCKS] if j in (0, WIDE - 1) else j - 1
        resist = aux_ref[at : at + 1, :]
        running = upstream + aux_ref[24 + at : 25 + at, :]
        head, flow = taken(row), taken(row + 1)
        if j in (0, WIDE - 1):
            beyond, edge, base = (
                (scen == 0, previous, upstream) if j == 0 else (scen == SCENS - 1, following, through)
            )
            resist = jnp.where(beyond, edge[0:1], resist)
            running = jnp.where(beyond, base + edge[1:2], running)
            head = jnp.where(beyond, outer_ref[0:SCENS, :], head)
            flow = jnp.where(beyond, outer_ref[SCENS:, :], flow)
        wide_ref[0, j] = first_head - running * scale + head
        wide_ref[1, j] = mean_flow + flow
        for state in range(4):
            wide_ref[2 + state, j] = none
        wide_ref[6, j] = jnp.broadcast_to(resist, (SCENS, LANES))

    def one_step(moment, carry):
        plan_rows = pl.ds(pl.multiple_of(moment * SCENS, SCENS), SCENS)
        head_left = plan_ref[0, plan_rows, :]
        small = plan_ref[1, plan_rows, :]
        large = plan_ref[2, plan_rows, :]

        def sent(j):
            head, flow = wide_ref[0, j], wide_ref[1, j]
            friction = wide_ref[6, j] * flow * jnp.abs(flow) + (
                (wide_ref[2, j] + wide_ref[3, j]) + (wide_ref[4, j] + wide_ref[5, j])
            )
            net = flow - friction
            return pltpu.roll(head + net, 1, 1), pltpu.roll(head - net, LANES - 1, 1)

        forward_before, (forward, backward) = None, sent(0)
        for j in range(WIDE):
            forward_after, backward_after = sent(j + 1) if j + 1 < WIDE else (forward, backward)
            if forward_before is None:
                forward_before = forward
            from_left = jnp.where(is_low, forward_before, forward)
            from_right = jnp.where(is_high, backward_after, backward)
            new_head = 0.5 * (from_left + from_right)
            new_flow = 0.5 * (from_left - from_right)
            if j == 1:
                new_head = jnp.where(at_first, head_left, new_head)
                new_flow = jnp.where(at_first, head_left - from_right, new_flow)
            if j == BLOCKS:
                new_head = jnp.where(at_last, from_left * small, new_head)
                new_flow = jnp.where(at_last, from_left * large, new_flow)
            change = new_flow - wide_ref[1, j]
            wide_ref[0, j] = new_head
            wide_ref[1, j] = new_flow
            for state in range(4):
                wide_ref[2 + state, j] = RETAINS[state] * wide_ref[2 + state, j] + SHARES[state] * change
            if 1 <= j <= BLOCKS:
                kept_ref[0, j - 1, plan_rows, :] = new_head
                kept_ref[1, j - 1, plan_rows, :] = new_flow
            forward_before, forward, backward = forward, forward_after, backward_after
        return carry

    lax.fori_loop(0, STEPS, one_step, 0)

    for field in range(2):
        for j in range(BLOCKS):
            for which in range(SCENS):
                piece = kept_ref[field, j, pl.ds(which, STEPS, stride=SCENS), :]
                cols_ref[field, which * STEPS : (which + 1) * STEPS, j * LANES : (j + 1) * LANES] = piece.astype(
                    jnp.bfloat16
                )
    total = None
    for field in range(2):
        columns = cols_ref[field]
        part = lax.dot_general(columns, columns, (((1,), (1,)), ((), ())), preferred_element_type=jnp.float32)
        total = part if total is None else total + part
    gram_ref[...] = total.reshape(SCENS, STEPS, COLS)


def fold_kernel(in_ref, out_ref):
    count, copies = in_ref.shape[0], out_ref.shape[0]
    total = in_ref[0]
    for which in range(1, count):
        total = total + in_ref[which]
    for which in range(copies):
        out_ref[which] = total


def basis_kernel(gram_ref, cols_ref, rows_ref, tri_ref, work_ref, out_ref, sems):
    scale = 1.0 / (2 * CELLS)
    sub = lax.broadcasted_iota(jnp.int32, (8, COLS), 0)
    lane = lax.broadcasted_iota(jnp.int32, (8, COLS), 1)
    groups = PANEL // 8
    work_ref[:, 0:COLS] = gram_ref[...].reshape(COLS, COLS) * scale
    for g in range(COLS // 8):
        work_ref[8 * g : 8 * g + 8, COLS:] = jnp.where(lane == sub + 8 * g, 1.0, 0.0).astype(jnp.float32)
    inverse_rows = []
    for low in range(0, COLS, PANEL):
        left = [work_ref[low + 8 * g : low + 8 * g + 8, 0:COLS] for g in range(groups)]
        right = [work_ref[low + 8 * g : low + 8 * g + 8, COLS:] for g in range(groups)]
        scaled = []
        for own in range(groups):
            start = low + 8 * own
            wide = {
                g: [jnp.broadcast_to(left[g][:, start + j : start + j + 1], (8, COLS)) for j in range(8)]
                for g in range(own, groups)
            }
            inverses = jnp.zeros((8, COLS), jnp.float32)
            for k in range(8):
                inverse = 1.0 / wide[own][k][k : k + 1, :]
                inverses = jnp.where(sub == k, inverse, inverses)
                ahead = {j: wide[own][j][k : k + 1, :] * inverse for j in range(k + 1, 8)}
                row_left = left[own][k : k + 1, :] * inverse
                row_right = right[own][k : k + 1, :] * inverse
                for g in range(own, groups):
                    factor = wide[g][k]
                    if g == own:
                        factor = jnp.where(sub > k, factor, 0.0)
                    for j in ahead:
                        wide[g][j] = wide[g][j] - factor * ahead[j]
                    left[g] = left[g] - factor * row_left
                    right[g] = right[g] - factor * row_right
            scaled.append(left[own] * inverses)
            root = jnp.sqrt(inverses)
            tri_ref[start : start + 8, :] = jnp.where(lane >= sub + start, left[own] * root, 0.0)
            inverse_rows.append(right[own] * root)
        if low + PANEL < COLS:
            update = lax.dot_general(
                jnp.concatenate(scaled, axis=0),
                jnp.concatenate([jnp.concatenate(left, axis=0), jnp.concatenate(right, axis=0)], axis=1),
                (((0,), (0,)), ((), ())),
                precision=EXACT,
                preferred_element_type=jnp.float32,
            )
            work_ref[low + PANEL :, :] = work_ref[low + PANEL :, :] - update[low + PANEL :, :]
    inverse = jnp.concatenate(inverse_rows, axis=0).T
    high = inverse.astype(jnp.bfloat16)
    rest = inverse - high.astype(jnp.float32)
    middle = rest.astype(jnp.bfloat16)
    both = jnp.concatenate([high, middle], axis=0)
    copies = []
    for field in range(2):
        for part in range(SHARE // CHUNK):
            piece = cols_ref[field, :, part * CHUNK : (part + 1) * CHUNK].T
            slot = len(copies)
            out_ref[slot] = jnp.dot(
                jnp.concatenate([piece, piece], axis=1), both, preferred_element_type=jnp.float32
            )
            copy = pltpu.make_async_copy(
                out_ref.at[slot], rows_ref.at[field, pl.ds(part * CHUNK, CHUNK), :], sems.at[slot]
            )
            copy.start()
            copies.append(copy)
    for copy in copies:
        copy.wait()


def fold(value, copies):
    return pl.pallas_call(
        fold_kernel,
        out_shape=jax.ShapeDtypeStruct((copies,) + value.shape[1:], jnp.float32),
        compiler_params=params(),
    )(value)


def exchanged(value, axis):
    return lax.all_to_all(value, axis, split_axis=0, concat_axis=0, tiled=True)


def local(perturb, resist, flow_rate, head_plan, valve_plan):
    f32 = jnp.float32
    vmem = pl.BlockSpec(memory_space=pltpu.VMEM)
    hbm = pl.BlockSpec(memory_space=pltpu.HBM)
    blocks = PART // LANES
    state = perturb.reshape(2, blocks, LANES).transpose(1, 0, 2).reshape(2 * blocks, LANES)
    resist = resist.reshape(LANES, LANES)
    edges, windows = pl.pallas_call(
        prepare_kernel,
        in_specs=[hbm] * 5,
        out_specs=(vmem, vmem),
        out_shape=(
            jax.ShapeDtypeStruct((REACHES, 4, LANES), f32),
            jax.ShapeDtypeStruct((SCENS, WINDOW, LANES), f32),
        ),
        scratch_shapes=[
            pltpu.VMEM((2 * blocks, LANES), f32),
            pltpu.VMEM((LANES, LANES), f32),
            pltpu.SMEM((1,), f32),
            pltpu.VMEM((1, STEPS), f32),
            pltpu.VMEM((1, STEPS), f32),
            pltpu.SemaphoreType.DMA((5,)),
        ],
        compiler_params=params(60),
    )(state, resist, flow_rate, head_plan, valve_plan)
    edges = exchanged(edges, "reach")
    aux = pl.pallas_call(
        spread_kernel, out_shape=jax.ShapeDtypeStruct((48, LANES), f32), compiler_params=params()
    )(resist)
    windows = exchanged(windows, "scen").reshape(SCENS * WINDOW, LANES)
    outer = pl.pallas_call(
        outer_kernel, out_shape=jax.ShapeDtypeStruct((2 * SCENS, LANES), f32), compiler_params=params()
    )(windows)
    top = (SCENS - 1) * REACHES
    pairs = [(top + r, r + 1) for r in range(REACHES - 1)]
    outer = lax.ppermute(outer, ("scen", "reach"), pairs + [(b, a) for a, b in pairs])
    columns, gram = pl.pallas_call(
        step_kernel,
        out_shape=(
            jax.ShapeDtypeStruct((2, COLS, SHARE), jnp.bfloat16),
            jax.ShapeDtypeStruct((SCENS, STEPS, COLS), f32),
        ),
        scratch_shapes=[
            pltpu.VMEM((7, WIDE, SCENS, LANES), f32),
            pltpu.VMEM((3, STEPS * SCENS, LANES), f32),
            pltpu.VMEM((2, BLOCKS, COLS, LANES), f32),
        ],
        compiler_params=params(),
    )(windows, outer, edges, aux)
    gram = fold(exchanged(gram, "scen"), REACHES)
    gram = fold(exchanged(gram, "reach"), SCENS)
    gram = exchanged(gram, "scen")
    chunks = 2 * SHARE // CHUNK
    return pl.pallas_call(
        basis_kernel,
        in_specs=[vmem, vmem],
        out_specs=(pl.BlockSpec(memory_space=pl.ANY), vmem),
        out_shape=(
            jax.ShapeDtypeStruct((2, SHARE, COLS), f32),
            jax.ShapeDtypeStruct((COLS, COLS), f32),
        ),
        scratch_shapes=[
            pltpu.VMEM((COLS, 2 * COLS), f32),
            pltpu.VMEM((chunks, CHUNK, COLS), f32),
            pltpu.SemaphoreType.DMA((chunks,)),
        ],
        compiler_params=params(),
    )(gram, columns)


def solution(mesh):
    in_specs = (P("scen", None, "reach"), P("reach"), P("scen"), P("scen", None), P("scen", None))
    out_specs = (P(None, ("reach", "scen"), None), P())
    return jax.shard_map(local, mesh=mesh, in_specs=in_specs, out_specs=out_specs, check_vma=False)
```

```python
import jax
import jax.numpy as jnp
from jax import lax
from jax.experimental import pallas as pl
from jax.experimental.pallas import tpu as pltpu
from jax.sharding import PartitionSpec as P

STEPS = 16
SHARES = (0.06, 0.04, 0.025, 0.015)
RETAINS = (0.2, 0.5, 0.8, 0.95)
LANES = 128
HALO = 16
SCENS = 8
REACHES = 64
RING = 8
COLS = SCENS * STEPS
CELLS = 1048576
PART = CELLS // REACHES
SHARE = PART // SCENS
BLOCKS = SHARE // LANES
RIGHT_ROW = 2 * BLOCKS
LEFT_ROW = RIGHT_ROW + 2
HEAD_ROW = LEFT_ROW + 2
VALVE_ROW = HEAD_ROW + 1
FLOW_ROW = VALVE_ROW + 1
WINDOW = 40
WIDE = BLOCKS + 2
PANEL = 64
CHUNK = 256
EXACT = lax.Precision.HIGHEST


def params(mib=40):
    return pltpu.CompilerParams(vmem_limit_bytes=mib * 1024 * 1024)


def edges_kernel(state_hbm, resist_hbm, out_ref, ends, resist, sems):
    rows = 2 * PART // LANES
    loads = [
        pltpu.make_async_copy(resist_hbm, resist, sems.at[0]),
        pltpu.make_async_copy(state_hbm.at[pl.ds(0, 8), :], ends.at[0], sems.at[1]),
        pltpu.make_async_copy(state_hbm.at[pl.ds(rows - 8, 8), :], ends.at[1], sems.at[2]),
    ]
    for copy in loads:
        copy.start()
    for copy in loads:
        copy.wait()
    lane = lax.broadcasted_iota(jnp.int32, (1, LANES), 1)
    total = jnp.sum(jnp.sum(resist[...], axis=0, keepdims=True), axis=1, keepdims=True)

    def both(first, final):
        return jnp.where(lane < HALO, first, jnp.where(lane >= LANES - HALO, final, 0.0))

    outer = both(resist[0:1, :], resist[LANES - 1 : LANES, :])
    upto = outer
    for step in (1, 2, 4, 8):
        upto = upto + jnp.where(lane >= step, pltpu.roll(upto, step, 1), 0.0)
    upto = jnp.where(lane < HALO, upto, upto - upto[:, LANES - 1 : LANES])
    upto = jnp.where((lane >= HALO) & (lane < LANES - HALO), total, upto)
    row = jnp.concatenate(
        [both(ends[0, 0:1, :], ends[1, 6:7, :]), both(ends[0, 1:2, :], ends[1, 7:8, :]), outer, upto], axis=0
    )
    out_ref[...] = jnp.broadcast_to(row[None], (REACHES, 4, LANES))


def window_kernel(state_ref, resist_ref, flow_ref, head_ref, valve_ref, out_ref, aux_ref):
    rows = 2 * BLOCKS
    none = jnp.zeros((2, LANES), jnp.float32)
    for which in range(SCENS):
        start = which * rows
        out_ref[which, 0:rows, :] = state_ref[start : start + rows, :]
        after = state_ref[start + rows : start + rows + 2, :] if which < SCENS - 1 else none
        out_ref[which, RIGHT_ROW : RIGHT_ROW + 2, :] = after
        out_ref[which, LEFT_ROW : LEFT_ROW + 2, :] = state_ref[start - 2 : start, :] if which > 0 else none
        out_ref[which, HEAD_ROW:WINDOW, :] = jnp.zeros((WINDOW - HEAD_ROW, LANES), jnp.float32)
        out_ref[which, HEAD_ROW : HEAD_ROW + 1, 0:STEPS] = head_ref[...]
        out_ref[which, VALVE_ROW : VALVE_ROW + 1, 0:STEPS] = valve_ref[...]
        out_ref[which, FLOW_ROW : FLOW_ROW + 1, :] = jnp.full((1, LANES), flow_ref[0], jnp.float32)

    scen = lax.axis_index("scen")
    first = scen * BLOCKS
    row_left = resist_ref[pl.ds(jnp.maximum(first - 1, 0), 1), :]
    row_right = resist_ref[pl.ds(jnp.minimum(first + BLOCKS, LANES - 1), 1), :]
    mine = resist_ref[pl.ds(pl.multiple_of(first, BLOCKS), BLOCKS), :]
    spread = jnp.concatenate([mine, row_right, row_left, jnp.zeros((6, LANES), jnp.float32)], axis=0)
    row_id = lax.broadcasted_iota(jnp.int32, (LANES, 1), 0)
    before = jnp.sum(jnp.where(row_id < first, resist_ref[...], 0.0), axis=0, keepdims=True)
    base = jnp.sum(before, axis=1, keepdims=True)
    a = lax.broadcasted_iota(jnp.int32, (LANES, LANES), 0)
    b = lax.broadcasted_iota(jnp.int32, (LANES, LANES), 1)
    upto = jnp.where(a <= b, 1.0, 0.0).astype(jnp.float32)
    inside = jnp.dot(spread, upto, precision=EXACT, preferred_element_type=jnp.float32)
    totals = jnp.sum(spread, axis=1, keepdims=True)
    c = lax.broadcasted_iota(jnp.int32, (24, 24), 0)
    d = lax.broadcasted_iota(jnp.int32, (24, 24), 1)
    ahead = jnp.where((d < c) & (c <= BLOCKS) & (d < BLOCKS), 1.0, 0.0)
    ahead = ahead - jnp.where((c == BLOCKS + 1) & (d == BLOCKS + 1), 1.0, 0.0)
    shift = jnp.dot(
        ahead.astype(jnp.float32),
        jnp.broadcast_to(totals, (24, LANES)),
        precision=EXACT,
        preferred_element_type=jnp.float32,
    )
    aux_ref[0:24, :] = spread
    aux_ref[24:48, :] = base + (shift + inside)


def patch_kernel(win_ref, edge_ref, out_ref):
    reach = lax.axis_index("reach")
    out_ref[0, LEFT_ROW : LEFT_ROW + 2, :] = edge_ref[jnp.maximum(reach - 1, 0), 0:2, :]
    out_ref[SCENS - 1, RIGHT_ROW : RIGHT_ROW + 2, :] = edge_ref[jnp.minimum(reach + 1, REACHES - 1), 0:2, :]


def step_kernel(win_ref, edge_ref, aux_ref, cols_ref, gram_ref, wide_ref, plan_ref, kept_ref):
    scen = lax.axis_index("scen")
    reach = lax.axis_index("reach")
    lane = lax.broadcasted_iota(jnp.int32, (SCENS, LANES), 1)
    at_first = (lane == 0) & (scen == 0) & (reach == 0)
    at_last = (lane == LANES - 1) & (scen == SCENS - 1) & (reach == REACHES - 1)
    is_low = lane == 0
    is_high = lane == LANES - 1

    def taken(row):
        return win_ref[pl.ds(row, SCENS, stride=WINDOW), :]

    head_plan = taken(HEAD_ROW)
    valve_plan = taken(VALVE_ROW)
    orifice = 1.0 / (1.0 + valve_plan)
    opened = valve_plan * orifice
    for moment in range(STEPS):
        for which, plan in enumerate((head_plan, orifice, opened)):
            plan_ref[which, moment * SCENS : (moment + 1) * SCENS, :] = jnp.broadcast_to(
                plan[:, moment : moment + 1], (SCENS, LANES)
            )
    steady = taken(FLOW_ROW)
    scale = steady * jnp.abs(steady) * (1.0 / CELLS)
    mean_flow = steady * CELLS ** (-0.5)
    first_head = plan_ref[0, 0:SCENS, :]
    place = lax.broadcasted_iota(jnp.int32, (REACHES, 1), 0)
    totals = edge_ref[:, 3, :]
    middle = slice(LANES // 2, LANES // 2 + 1)
    upstream = jnp.sum(jnp.where(place < reach, totals, 0.0), axis=0, keepdims=True)[:, middle]
    through = jnp.sum(jnp.where(place <= reach, totals, 0.0), axis=0, keepdims=True)[:, middle]
    previous = edge_ref[jnp.maximum(reach - 1, 0)]
    following = edge_ref[jnp.minimum(reach + 1, REACHES - 1)]
    none = jnp.zeros((SCENS, LANES), jnp.float32)
    for j in range(WIDE):
        row = [LEFT_ROW, RIGHT_ROW][j > BLOCKS] if j in (0, WIDE - 1) else 2 * (j - 1)
        at = [BLOCKS + 1, BLOCKS][j > BLOCKS] if j in (0, WIDE - 1) else j - 1
        resist = aux_ref[at : at + 1, :]
        running = upstream + aux_ref[24 + at : 25 + at, :]
        head, flow = taken(row), taken(row + 1)
        if j in (0, WIDE - 1):
            beyond, edge, base = (
                (scen == 0, previous, upstream) if j == 0 else (scen == SCENS - 1, following, through)
            )
            resist = jnp.where(beyond, edge[2:3], resist)
            running = jnp.where(beyond, base + edge[3:4], running)
        wide_ref[0, j] = first_head - running * scale + head
        wide_ref[1, j] = mean_flow + flow
        for state in range(4):
            wide_ref[2 + state, j] = none
        wide_ref[6, j] = jnp.broadcast_to(resist, (SCENS, LANES))

    def one_step(moment, carry):
        plan_rows = pl.ds(pl.multiple_of(moment * SCENS, SCENS), SCENS)
        head_left = plan_ref[0, plan_rows, :]
        small = plan_ref[1, plan_rows, :]
        large = plan_ref[2, plan_rows, :]

        def sent(j):
            head, flow = wide_ref[0, j], wide_ref[1, j]
            friction = wide_ref[6, j] * flow * jnp.abs(flow) + (
                (wide_ref[2, j] + wide_ref[3, j]) + (wide_ref[4, j] + wide_ref[5, j])
            )
            net = flow - friction
            return pltpu.roll(head + net, 1, 1), pltpu.roll(head - net, LANES - 1, 1)

        forward_before, (forward, backward) = None, sent(0)
        for j in range(WIDE):
            forward_after, backward_after = sent(j + 1) if j + 1 < WIDE else (forward, backward)
            if forward_before is None:
                forward_before = forward
            from_left = jnp.where(is_low, forward_before, forward)
            from_right = jnp.where(is_high, backward_after, backward)
            new_head = 0.5 * (from_left + from_right)
            new_flow = 0.5 * (from_left - from_right)
            if j == 1:
                new_head = jnp.where(at_first, head_left, new_head)
                new_flow = jnp.where(at_first, head_left - from_right, new_flow)
            if j == BLOCKS:
                new_head = jnp.where(at_last, from_left * small, new_head)
                new_flow = jnp.where(at_last, from_left * large, new_flow)
            change = new_flow - wide_ref[1, j]
            wide_ref[0, j] = new_head
            wide_ref[1, j] = new_flow
            for state in range(4):
                wide_ref[2 + state, j] = RETAINS[state] * wide_ref[2 + state, j] + SHARES[state] * change
            if 1 <= j <= BLOCKS:
                kept_ref[0, j - 1, plan_rows, :] = new_head
                kept_ref[1, j - 1, plan_rows, :] = new_flow
            forward_before, forward, backward = forward, forward_after, backward_after
        return carry

    lax.fori_loop(0, STEPS, one_step, 0)

    for field in range(2):
        for j in range(BLOCKS):
            for which in range(SCENS):
                piece = kept_ref[field, j, pl.ds(which, STEPS, stride=SCENS), :]
                cols_ref[field, which * STEPS : (which + 1) * STEPS, j * LANES : (j + 1) * LANES] = piece.astype(
                    jnp.bfloat16
                )
    total = None
    for field in range(2):
        columns = cols_ref[field]
        part = lax.dot_general(columns, columns, (((1,), (1,)), ((), ())), preferred_element_type=jnp.float32)
        total = part if total is None else total + part
    gram_ref[...] = total.reshape(SCENS, STEPS, COLS)


def fold_kernel(in_ref, out_ref):
    count, copies = in_ref.shape[0], out_ref.shape[0]
    total = in_ref[0]
    for which in range(1, count):
        total = total + in_ref[which]
    for which in range(copies):
        out_ref[which] = total


def basis_kernel(gram_ref, cols_ref, rows_ref, tri_ref, work_ref, out_ref, sems):
    scale = 1.0 / (2 * CELLS)
    sub = lax.broadcasted_iota(jnp.int32, (8, COLS), 0)
    lane = lax.broadcasted_iota(jnp.int32, (8, COLS), 1)
    groups = PANEL // 8
    work_ref[:, 0:COLS] = gram_ref[...].reshape(COLS, COLS) * scale
    for g in range(COLS // 8):
        work_ref[8 * g : 8 * g + 8, COLS:] = jnp.where(lane == sub + 8 * g, 1.0, 0.0).astype(jnp.float32)
    inverse_rows = []
    for low in range(0, COLS, PANEL):
        left = [work_ref[low + 8 * g : low + 8 * g + 8, 0:COLS] for g in range(groups)]
        right = [work_ref[low + 8 * g : low + 8 * g + 8, COLS:] for g in range(groups)]
        scaled = []
        for own in range(groups):
            start = low + 8 * own
            wide = {
                g: [jnp.broadcast_to(left[g][:, start + j : start + j + 1], (8, COLS)) for j in range(8)]
                for g in range(own, groups)
            }
            inverses = jnp.zeros((8, COLS), jnp.float32)
            for k in range(8):
                inverse = 1.0 / wide[own][k][k : k + 1, :]
                inverses = jnp.where(sub == k, inverse, inverses)
                ahead = {j: wide[own][j][k : k + 1, :] * inverse for j in range(k + 1, 8)}
                row_left = left[own][k : k + 1, :] * inverse
                row_right = right[own][k : k + 1, :] * inverse
                for g in range(own, groups):
                    factor = wide[g][k]
                    if g == own:
                        factor = jnp.where(sub > k, factor, 0.0)
                    for j in ahead:
                        wide[g][j] = wide[g][j] - factor * ahead[j]
                    left[g] = left[g] - factor * row_left
                    right[g] = right[g] - factor * row_right
            scaled.append(left[own] * inverses)
            root = jnp.sqrt(inverses)
            tri_ref[start : start + 8, :] = jnp.where(lane >= sub + start, left[own] * root, 0.0)
            inverse_rows.append(right[own] * root)
        if low + PANEL < COLS:
            update = lax.dot_general(
                jnp.concatenate(scaled, axis=0),
                jnp.concatenate([jnp.concatenate(left, axis=0), jnp.concatenate(right, axis=0)], axis=1),
                (((0,), (0,)), ((), ())),
                precision=EXACT,
                preferred_element_type=jnp.float32,
            )
            work_ref[low + PANEL :, :] = work_ref[low + PANEL :, :] - update[low + PANEL :, :]
    inverse = jnp.concatenate(inverse_rows, axis=0).T
    high = inverse.astype(jnp.bfloat16)
    rest = inverse - high.astype(jnp.float32)
    middle = rest.astype(jnp.bfloat16)
    both = jnp.concatenate([high, middle], axis=0)
    copies = []
    for field in range(2):
        for part in range(SHARE // CHUNK):
            piece = cols_ref[field, :, part * CHUNK : (part + 1) * CHUNK].T
            slot = len(copies)
            out_ref[slot] = jnp.dot(
                jnp.concatenate([piece, piece], axis=1), both, preferred_element_type=jnp.float32
            )
            copy = pltpu.make_async_copy(
                out_ref.at[slot], rows_ref.at[field, pl.ds(part * CHUNK, CHUNK), :], sems.at[slot]
            )
            copy.start()
            copies.append(copy)
    for copy in copies:
        copy.wait()


def fold(value, copies):
    return pl.pallas_call(
        fold_kernel,
        out_shape=jax.ShapeDtypeStruct((copies,) + value.shape[1:], jnp.float32),
        compiler_params=params(),
    )(value)


def exchanged(value, axis, groups=None):
    return lax.all_to_all(value, axis, split_axis=0, concat_axis=0, axis_index_groups=groups, tiled=True)


def local(perturb, resist, flow_rate, head_plan, valve_plan):
    f32 = jnp.float32
    vmem = pl.BlockSpec(memory_space=pltpu.VMEM)
    smem = pl.BlockSpec(memory_space=pltpu.SMEM)
    hbm = pl.BlockSpec(memory_space=pltpu.HBM)
    blocks = PART // LANES
    state = perturb.reshape(2, blocks, LANES).transpose(1, 0, 2).reshape(2 * blocks, LANES)
    resist = resist.reshape(LANES, LANES)
    edges = pl.pallas_call(
        edges_kernel,
        in_specs=[hbm, hbm],
        out_specs=vmem,
        out_shape=jax.ShapeDtypeStruct((REACHES, 4, LANES), f32),
        scratch_shapes=[
            pltpu.VMEM((2, 8, LANES), f32),
            pltpu.VMEM((LANES, LANES), f32),
            pltpu.SemaphoreType.DMA((3,)),
        ],
        compiler_params=params(61),
    )(state, resist)
    edges = exchanged(edges, "reach")
    windows, aux = pl.pallas_call(
        window_kernel,
        in_specs=[vmem, vmem, smem, vmem, vmem],
        out_shape=(
            jax.ShapeDtypeStruct((SCENS, WINDOW, LANES), f32),
            jax.ShapeDtypeStruct((48, LANES), f32),
        ),
        compiler_params=params(),
    )(state, resist, flow_rate, head_plan, valve_plan)
    windows = pl.pallas_call(
        patch_kernel,
        in_specs=[vmem, vmem],
        out_specs=vmem,
        out_shape=jax.ShapeDtypeStruct((SCENS, WINDOW, LANES), f32),
        input_output_aliases={0: 0},
        compiler_params=params(),
    )(windows, edges)
    windows = exchanged(windows, "scen").reshape(SCENS * WINDOW, LANES)
    columns, gram = pl.pallas_call(
        step_kernel,
        out_shape=(
            jax.ShapeDtypeStruct((2, COLS, SHARE), jnp.bfloat16),
            jax.ShapeDtypeStruct((SCENS, STEPS, COLS), f32),
        ),
        scratch_shapes=[
            pltpu.VMEM((7, WIDE, SCENS, LANES), f32),
            pltpu.VMEM((3, STEPS * SCENS, LANES), f32),
            pltpu.VMEM((2, BLOCKS, COLS, LANES), f32),
        ],
        compiler_params=params(),
    )(windows, edges, aux)
    along = [[RING * a + b for b in range(RING)] for a in range(RING)]
    across = [[RING * b + a for b in range(RING)] for a in range(RING)]
    gram = fold(exchanged(gram, "scen"), RING)
    gram = fold(exchanged(gram, "reach", along), RING)
    gram = fold(exchanged(gram, "reach", across), SCENS)
    gram = exchanged(gram, "scen")
    chunks = 2 * SHARE // CHUNK
    return pl.pallas_call(
        basis_kernel,
        in_specs=[vmem, vmem],
        out_specs=(pl.BlockSpec(memory_space=pl.ANY), vmem),
        out_shape=(
            jax.ShapeDtypeStruct((2, SHARE, COLS), f32),
            jax.ShapeDtypeStruct((COLS, COLS), f32),
        ),
        scratch_shapes=[
            pltpu.VMEM((COLS, 2 * COLS), f32),
            pltpu.VMEM((chunks, CHUNK, COLS), f32),
            pltpu.SemaphoreType.DMA((chunks,)),
        ],
        compiler_params=params(),
    )(gram, columns)


def solution(mesh):
    in_specs = (P("scen", None, "reach"), P("reach"), P("scen"), P("scen", None), P("scen", None))
    out_specs = (P(None, ("reach", "scen"), None), P())
    return jax.shard_map(local, mesh=mesh, in_specs=in_specs, out_specs=out_specs, check_vma=False)
```

```python
import jax
import jax.numpy as jnp
from jax import lax
from jax.experimental import pallas as pl
from jax.experimental.pallas import tpu as pltpu
from jax.sharding import PartitionSpec as P

STEPS = 16
SHARES = (0.06, 0.04, 0.025, 0.015)
RETAINS = (0.2, 0.5, 0.8, 0.95)
LANES = 128
HALO = 16
SCENS = 8
REACHES = 64
RING = 8
COLS = SCENS * STEPS
CELLS = 1048576
PART = CELLS // REACHES
SHARE = PART // SCENS
BLOCKS = SHARE // LANES
RIGHT_ROW = 2 * BLOCKS
LEFT_ROW = RIGHT_ROW + 2
HEAD_ROW = LEFT_ROW + 2
VALVE_ROW = HEAD_ROW + 1
FLOW_ROW = VALVE_ROW + 1
WINDOW = 40
WIDE = BLOCKS + 2
PANEL = 64
CHUNK = 256
HALF = COLS // 2
QUARTER = COLS // 4
PIECES = 3
EXACT = lax.Precision.HIGHEST


def params(mib=40):
    return pltpu.CompilerParams(vmem_limit_bytes=mib * 1024 * 1024)


def edges_kernel(state_hbm, resist_hbm, out_ref, ends, resist, sems):
    rows = 2 * PART // LANES
    loads = [
        pltpu.make_async_copy(resist_hbm, resist, sems.at[0]),
        pltpu.make_async_copy(state_hbm.at[pl.ds(0, 8), :], ends.at[0], sems.at[1]),
        pltpu.make_async_copy(state_hbm.at[pl.ds(rows - 8, 8), :], ends.at[1], sems.at[2]),
    ]
    for copy in loads:
        copy.start()
    for copy in loads:
        copy.wait()
    lane = lax.broadcasted_iota(jnp.int32, (1, LANES), 1)
    is_first, is_final = lane < HALO, lane >= LANES - HALO
    total = jnp.sum(jnp.sum(resist[...], axis=0, keepdims=True), axis=1, keepdims=True)
    outer = jnp.where(is_first, resist[0:1, :], jnp.where(is_final, resist[LANES - 1 : LANES, :], 0.0))
    upto = outer
    for step in (1, 2, 4, 8):
        upto = upto + jnp.where(lane >= step, pltpu.roll(upto, step, 1), 0.0)
    back = jnp.where(lane == LANES - 1, total, upto - upto[:, LANES - 1 : LANES])
    firsts = (ends[0, 0:1, :], ends[0, 1:2, :], resist[0:1, :], upto)
    finals = (ends[1, 6:7, :], ends[1, 7:8, :], resist[LANES - 1 : LANES, :], back)
    row = jnp.zeros((1, LANES), jnp.float32)
    for place, (first, final) in enumerate(zip(firsts, finals)):
        low, high = jnp.where(is_first, first, 0.0), jnp.where(is_final, final, 0.0)
        if place:
            low, high = pltpu.roll(low, place * HALO, 1), pltpu.roll(high, LANES - place * HALO, 1)
        row = row + low + high
    out_ref[...] = jnp.broadcast_to(row[None], (REACHES, 1, LANES))


def last_of(row, place):
    lane = lax.broadcasted_iota(jnp.int32, (1, LANES), 1)
    moved = pltpu.roll(row, place * HALO, 1) if place else row
    return jnp.where(lane >= LANES - HALO, moved, 0.0)


def first_of(row, place):
    lane = lax.broadcasted_iota(jnp.int32, (1, LANES), 1)
    moved = pltpu.roll(row, LANES - place * HALO, 1) if place else row
    return jnp.where(lane < HALO, moved, 0.0)


def window_kernel(state_ref, resist_ref, flow_ref, head_ref, valve_ref, out_ref, aux_ref):
    rows = 2 * BLOCKS
    none = jnp.zeros((2, LANES), jnp.float32)
    for which in range(SCENS):
        start = which * rows
        out_ref[which, 0:rows, :] = state_ref[start : start + rows, :]
        after = state_ref[start + rows : start + rows + 2, :] if which < SCENS - 1 else none
        out_ref[which, RIGHT_ROW : RIGHT_ROW + 2, :] = after
        out_ref[which, LEFT_ROW : LEFT_ROW + 2, :] = state_ref[start - 2 : start, :] if which > 0 else none
        out_ref[which, HEAD_ROW:WINDOW, :] = jnp.zeros((WINDOW - HEAD_ROW, LANES), jnp.float32)
        out_ref[which, HEAD_ROW : HEAD_ROW + 1, 0:STEPS] = head_ref[...]
        out_ref[which, VALVE_ROW : VALVE_ROW + 1, 0:STEPS] = valve_ref[...]
        out_ref[which, FLOW_ROW : FLOW_ROW + 1, :] = jnp.full((1, LANES), flow_ref[0], jnp.float32)

    scen = lax.axis_index("scen")
    first = scen * BLOCKS
    row_left = resist_ref[pl.ds(jnp.maximum(first - 1, 0), 1), :]
    row_right = resist_ref[pl.ds(jnp.minimum(first + BLOCKS, LANES - 1), 1), :]
    mine = resist_ref[pl.ds(pl.multiple_of(first, BLOCKS), BLOCKS), :]
    spread = jnp.concatenate([mine, row_right, row_left, jnp.zeros((6, LANES), jnp.float32)], axis=0)
    row_id = lax.broadcasted_iota(jnp.int32, (LANES, 1), 0)
    before = jnp.sum(jnp.where(row_id < first, resist_ref[...], 0.0), axis=0, keepdims=True)
    base = jnp.sum(before, axis=1, keepdims=True)
    a = lax.broadcasted_iota(jnp.int32, (LANES, LANES), 0)
    b = lax.broadcasted_iota(jnp.int32, (LANES, LANES), 1)
    upto = jnp.where(a <= b, 1.0, 0.0).astype(jnp.float32)
    inside = jnp.dot(spread, upto, precision=EXACT, preferred_element_type=jnp.float32)
    totals = jnp.sum(spread, axis=1, keepdims=True)
    c = lax.broadcasted_iota(jnp.int32, (24, 24), 0)
    d = lax.broadcasted_iota(jnp.int32, (24, 24), 1)
    ahead = jnp.where((d < c) & (c <= BLOCKS) & (d < BLOCKS), 1.0, 0.0)
    ahead = ahead - jnp.where((c == BLOCKS + 1) & (d == BLOCKS + 1), 1.0, 0.0)
    shift = jnp.dot(
        ahead.astype(jnp.float32),
        jnp.broadcast_to(totals, (24, LANES)),
        precision=EXACT,
        preferred_element_type=jnp.float32,
    )
    aux_ref[0:24, :] = spread
    aux_ref[24:48, :] = base + (shift + inside)


def patch_kernel(win_ref, edge_ref, out_ref):
    reach = lax.axis_index("reach")
    previous = edge_ref[jnp.maximum(reach - 1, 0)]
    following = edge_ref[jnp.minimum(reach + 1, REACHES - 1)]
    for field in range(2):
        out_ref[0, LEFT_ROW + field : LEFT_ROW + field + 1, :] = last_of(previous, field)
        out_ref[SCENS - 1, RIGHT_ROW + field : RIGHT_ROW + field + 1, :] = first_of(following, field)


def step_kernel(win_ref, edge_ref, aux_ref, cols_ref, gram_ref, wide_ref, plan_ref, kept_ref, order_ref):
    scen = lax.axis_index("scen")
    reach = lax.axis_index("reach")
    lane = lax.broadcasted_iota(jnp.int32, (SCENS, LANES), 1)
    at_first = (lane == 0) & (scen == 0) & (reach == 0)
    at_last = (lane == LANES - 1) & (scen == SCENS - 1) & (reach == REACHES - 1)
    is_low = lane == 0
    is_high = lane == LANES - 1

    def taken(row):
        return win_ref[pl.ds(row, SCENS, stride=WINDOW), :]

    head_plan = taken(HEAD_ROW)
    valve_plan = taken(VALVE_ROW)
    orifice = 1.0 / (1.0 + valve_plan)
    opened = valve_plan * orifice
    for moment in range(STEPS):
        for which, plan in enumerate((head_plan, orifice, opened)):
            plan_ref[which, moment * SCENS : (moment + 1) * SCENS, :] = jnp.broadcast_to(
                plan[:, moment : moment + 1], (SCENS, LANES)
            )
    steady = taken(FLOW_ROW)
    scale = steady * jnp.abs(steady) * (1.0 / CELLS)
    mean_flow = steady * CELLS ** (-0.5)
    first_head = plan_ref[0, 0:SCENS, :]
    place = lax.broadcasted_iota(jnp.int32, (REACHES, 1, LANES), 0)
    held = edge_ref[...]
    at_total = slice(LANES - 3 * HALO - 1, LANES - 3 * HALO)
    upstream = jnp.sum(jnp.where(place < reach, held, 0.0), axis=0)[:, at_total]
    through = jnp.sum(jnp.where(place <= reach, held, 0.0), axis=0)[:, at_total]
    previous = edge_ref[jnp.maximum(reach - 1, 0)]
    following = edge_ref[jnp.minimum(reach + 1, REACHES - 1)]
    none = jnp.zeros((SCENS, LANES), jnp.float32)
    for j in range(WIDE):
        row = [LEFT_ROW, RIGHT_ROW][j > BLOCKS] if j in (0, WIDE - 1) else 2 * (j - 1)
        at = [BLOCKS + 1, BLOCKS][j > BLOCKS] if j in (0, WIDE - 1) else j - 1
        resist = aux_ref[at : at + 1, :]
        running = upstream + aux_ref[24 + at : 25 + at, :]
        head, flow = taken(row), taken(row + 1)
        if j in (0, WIDE - 1):
            if j == 0:
                beyond, base = scen == 0, upstream
                edge, upto = last_of(previous, 2), last_of(previous, 3)
                upto = jnp.where(is_high[0:1], 0.0, upto)
            else:
                beyond, base = scen == SCENS - 1, through
                edge, upto = first_of(following, 2), first_of(following, 3)
            resist = jnp.where(beyond, edge, resist)
            running = jnp.where(beyond, base + upto, running)
        wide_ref[0, j] = first_head - running * scale + head
        wide_ref[1, j] = mean_flow + flow
        for state in range(4):
            wide_ref[2 + state, j] = none
        wide_ref[6, j] = jnp.broadcast_to(resist, (SCENS, LANES))

    def two_steps(pair, carry):
        for half in range(2):
            plan_rows = pl.ds(pl.multiple_of((2 * pair + half) * SCENS, SCENS), SCENS)
            head_left = plan_ref[0, plan_rows, :]
            small = plan_ref[1, plan_rows, :]
            large = plan_ref[2, plan_rows, :]

            def sent(j):
                head, flow = wide_ref[0, j], wide_ref[1, j]
                friction = wide_ref[6, j] * flow * jnp.abs(flow) + (
                    (wide_ref[2, j] + wide_ref[3, j]) + (wide_ref[4, j] + wide_ref[5, j])
                )
                net = flow - friction
                return pltpu.roll(head + net, 1, 1), pltpu.roll(head - net, LANES - 1, 1)

            forward_before, (forward, backward) = None, sent(0)
            for j in range(WIDE):
                forward_after, backward_after = sent(j + 1) if j + 1 < WIDE else (forward, backward)
                if forward_before is None:
                    forward_before = forward
                from_left = jnp.where(is_low, forward_before, forward)
                from_right = jnp.where(is_high, backward_after, backward)
                new_head = 0.5 * (from_left + from_right)
                new_flow = 0.5 * (from_left - from_right)
                if j == 1:
                    new_head = jnp.where(at_first, head_left, new_head)
                    new_flow = jnp.where(at_first, head_left - from_right, new_flow)
                if j == BLOCKS:
                    new_head = jnp.where(at_last, from_left * small, new_head)
                    new_flow = jnp.where(at_last, from_left * large, new_flow)
                change = new_flow - wide_ref[1, j]
                wide_ref[0, j] = new_head
                wide_ref[1, j] = new_flow
                for state in range(4):
                    wide_ref[2 + state, j] = RETAINS[state] * wide_ref[2 + state, j] + SHARES[state] * change
                if 1 <= j <= BLOCKS:
                    for field, value in enumerate((new_head, new_flow)):
                        if half == 0:
                            kept_ref[field, j - 1] = value
                        else:
                            both = jnp.concatenate([kept_ref[field, j - 1], value], axis=0)
                            cols_ref[
                                field,
                                pl.ds(pl.multiple_of(pair * 2 * SCENS, 2 * SCENS), 2 * SCENS),
                                (j - 1) * LANES : j * LANES,
                            ] = both.astype(jnp.bfloat16)
                forward_before, forward, backward = forward, forward_after, backward_after
        return carry

    lax.fori_loop(0, STEPS // 2, two_steps, 0)

    total = None
    for field in range(2):
        columns = cols_ref[field]
        part = lax.dot_general(columns, columns, (((1,), (1,)), ((), ())), preferred_element_type=jnp.float32)
        total = part if total is None else total + part
    order_ref[...] = total
    rows = [order_ref[pl.ds(which, STEPS, stride=SCENS), :] for which in range(SCENS)]
    order_ref[...] = jnp.concatenate(rows, axis=0).T
    rows = [order_ref[pl.ds(which, STEPS, stride=SCENS), :] for which in range(SCENS)]
    high = lax.broadcasted_iota(jnp.int32, (QUARTER, COLS), 1) >= HALF
    upper, lower = jnp.concatenate(rows[4:6], axis=0), jnp.concatenate(rows[6:8], axis=0)
    packed = jnp.concatenate(rows[0:4] + [jnp.where(high, upper, pltpu.roll(lower, HALF, 1))], axis=0)
    for which in range(SCENS):
        for part in range(PIECES):
            at = (which * PIECES + part) * 4
            gram_ref[which, part] = packed[at : at + 4, :]


def fold_kernel(in_ref, out_ref):
    count, copies = in_ref.shape[0], out_ref.shape[0]
    total = in_ref[0]
    for which in range(1, count):
        total = total + in_ref[which]
    for which in range(copies):
        out_ref[which] = total


def basis_kernel(gram_ref, cols_ref, rows_ref, tri_ref, work_ref, turned_ref, order_ref, out_ref, sems):
    scale = 1.0 / (2 * CELLS)
    sub = lax.broadcasted_iota(jnp.int32, (8, COLS), 0)
    lane = lax.broadcasted_iota(jnp.int32, (8, COLS), 1)
    groups = PANEL // 8
    for field in range(2):
        for part in range(SHARE // CHUNK):
            turned_ref[field * (SHARE // CHUNK) + part] = cols_ref[field, :, part * CHUNK : (part + 1) * CHUNK].T
    for which in range(SCENS):
        for part in range(PIECES):
            at = (which * PIECES + part) * 4
            work_ref[at : at + 4, 0:COLS] = gram_ref[which, part] * scale
    work_ref[HALF + QUARTER :, 0:COLS] = pltpu.roll(work_ref[HALF : HALF + QUARTER, 0:COLS], HALF, 1)
    for g in range(COLS // 8):
        work_ref[8 * g : 8 * g + 8, COLS:] = jnp.where(lane == sub + 8 * g, 1.0, 0.0).astype(jnp.float32)
    inverse_rows = []
    for low in range(0, COLS, PANEL):
        left = [work_ref[low + 8 * g : low + 8 * g + 8, 0:COLS] for g in range(groups)]
        right = [work_ref[low + 8 * g : low + 8 * g + 8, COLS:] for g in range(groups)]
        scaled = []
        for own in range(groups):
            start = low + 8 * own
            wide = {
                g: [jnp.broadcast_to(left[g][:, start + j : start + j + 1], (8, COLS)) for j in range(8)]
                for g in range(own, groups)
            }
            inverses = jnp.zeros((8, COLS), jnp.float32)
            for k in range(8):
                inverse = 1.0 / wide[own][k][k : k + 1, :]
                inverses = jnp.where(sub == k, inverse, inverses)
                ahead = {j: wide[own][j][k : k + 1, :] * inverse for j in range(k + 1, 8)}
                row_left = left[own][k : k + 1, :] * inverse
                row_right = right[own][k : k + 1, :] * inverse
                for g in range(own, groups):
                    factor = wide[g][k]
                    if g == own:
                        factor = jnp.where(sub > k, factor, 0.0)
                    for j in ahead:
                        wide[g][j] = wide[g][j] - factor * ahead[j]
                    left[g] = left[g] - factor * row_left
                    right[g] = right[g] - factor * row_right
            scaled.append(left[own] * inverses)
            root = jnp.sqrt(inverses)
            tri_ref[start : start + 8, :] = jnp.where(lane >= sub + start, left[own] * root, 0.0)
            inverse_rows.append(right[own] * root)
        if low + PANEL < COLS:
            update = lax.dot_general(
                jnp.concatenate(scaled, axis=0),
                jnp.concatenate([jnp.concatenate(left, axis=0), jnp.concatenate(right, axis=0)], axis=1),
                (((0,), (0,)), ((), ())),
                precision=EXACT,
                preferred_element_type=jnp.float32,
            )
            work_ref[low + PANEL :, :] = work_ref[low + PANEL :, :] - update[low + PANEL :, :]
    order_ref[...] = jnp.concatenate(inverse_rows, axis=0).T
    inverse = jnp.concatenate([order_ref[pl.ds(n, SCENS, stride=STEPS), :] for n in range(STEPS)], axis=0)
    high = inverse.astype(jnp.bfloat16)
    rest = inverse - high.astype(jnp.float32)
    middle = rest.astype(jnp.bfloat16)
    both = jnp.concatenate([high, middle], axis=0)
    copies = []
    for field in range(2):
        for part in range(SHARE // CHUNK):
            slot = len(copies)
            piece = turned_ref[slot]
            out_ref[slot] = jnp.dot(
                jnp.concatenate([piece, piece], axis=1), both, preferred_element_type=jnp.float32
            )
            copy = pltpu.make_async_copy(
                out_ref.at[slot], rows_ref.at[field, pl.ds(part * CHUNK, CHUNK), :], sems.at[slot]
            )
            copy.start()
            copies.append(copy)
    for copy in copies:
        copy.wait()


def fold(value, copies):
    return pl.pallas_call(
        fold_kernel,
        out_shape=jax.ShapeDtypeStruct((copies,) + value.shape[1:], jnp.float32),
        compiler_params=params(),
    )(value)


def exchanged(value, axis, groups=None):
    return lax.all_to_all(value, axis, split_axis=0, concat_axis=0, axis_index_groups=groups, tiled=True)


def local(perturb, resist, flow_rate, head_plan, valve_plan):
    f32 = jnp.float32
    vmem = pl.BlockSpec(memory_space=pltpu.VMEM)
    smem = pl.BlockSpec(memory_space=pltpu.SMEM)
    hbm = pl.BlockSpec(memory_space=pltpu.HBM)
    blocks = PART // LANES
    state = perturb.reshape(2, blocks, LANES).transpose(1, 0, 2).reshape(2 * blocks, LANES)
    resist = resist.reshape(LANES, LANES)
    edges = pl.pallas_call(
        edges_kernel,
        in_specs=[hbm, hbm],
        out_specs=vmem,
        out_shape=jax.ShapeDtypeStruct((REACHES, 1, LANES), f32),
        scratch_shapes=[
            pltpu.VMEM((2, 8, LANES), f32),
            pltpu.VMEM((LANES, LANES), f32),
            pltpu.SemaphoreType.DMA((3,)),
        ],
        compiler_params=params(61),
    )(state, resist)
    edges = exchanged(edges, "reach")
    windows, aux = pl.pallas_call(
        window_kernel,
        in_specs=[vmem, vmem, smem, vmem, vmem],
        out_shape=(
            jax.ShapeDtypeStruct((SCENS, WINDOW, LANES), f32),
            jax.ShapeDtypeStruct((48, LANES), f32),
        ),
        compiler_params=params(),
    )(state, resist, flow_rate, head_plan, valve_plan)
    windows = pl.pallas_call(
        patch_kernel,
        in_specs=[vmem, vmem],
        out_specs=vmem,
        out_shape=jax.ShapeDtypeStruct((SCENS, WINDOW, LANES), f32),
        input_output_aliases={0: 0},
        compiler_params=params(),
    )(windows, edges)
    windows = exchanged(windows, "scen").reshape(SCENS * WINDOW, LANES)
    columns, gram = pl.pallas_call(
        step_kernel,
        out_shape=(
            jax.ShapeDtypeStruct((2, COLS, SHARE), jnp.bfloat16),
            jax.ShapeDtypeStruct((SCENS, PIECES, 4, COLS), f32),
        ),
        scratch_shapes=[
            pltpu.VMEM((7, WIDE, SCENS, LANES), f32),
            pltpu.VMEM((3, STEPS * SCENS, LANES), f32),
            pltpu.VMEM((2, BLOCKS, SCENS, LANES), f32),
            pltpu.VMEM((COLS, COLS), f32),
        ],
        compiler_params=params(),
    )(windows, edges, aux)
    along = [[RING * a + b for b in range(RING)] for a in range(RING)]
    across = [[RING * b + a for b in range(RING)] for a in range(RING)]
    gram = fold(exchanged(gram, "scen"), RING)
    gram = fold(exchanged(gram, "reach", along), RING)
    gram = fold(exchanged(gram, "reach", across), SCENS)
    gram = exchanged(gram, "scen")
    chunks = 2 * SHARE // CHUNK
    return pl.pallas_call(
        basis_kernel,
        in_specs=[vmem, vmem],
        out_specs=(pl.BlockSpec(memory_space=pl.ANY), vmem),
        out_shape=(
            jax.ShapeDtypeStruct((2, SHARE, COLS), f32),
            jax.ShapeDtypeStruct((COLS, COLS), f32),
        ),
        scratch_shapes=[
            pltpu.VMEM((COLS, 2 * COLS), f32),
            pltpu.VMEM((chunks, CHUNK, COLS), jnp.bfloat16),
            pltpu.VMEM((COLS, COLS), f32),
            pltpu.VMEM((chunks, CHUNK, COLS), f32),
            pltpu.SemaphoreType.DMA((chunks,)),
        ],
        compiler_params=params(),
    )(gram, columns)


def solution(mesh):
    in_specs = (P("scen", None, "reach"), P("reach"), P("scen"), P("scen", None), P("scen", None))
    out_specs = (P(None, ("reach", "scen"), None), P())
    return jax.shard_map(local, mesh=mesh, in_specs=in_specs, out_specs=out_specs, check_vma=False)
```

```python
import jax
import jax.numpy as jnp
from jax import lax
from jax.experimental import pallas as pl
from jax.experimental.pallas import tpu as pltpu
from jax.sharding import PartitionSpec as P

STEPS = 16
SHARES = (0.06, 0.04, 0.025, 0.015)
RETAINS = (0.2, 0.5, 0.8, 0.95)
LANES = 128
HALO = 16
SCENS = 8
REACHES = 64
RING = 8
COLS = SCENS * STEPS
CELLS = 1048576
PART = CELLS // REACHES
SHARE = PART // SCENS
BLOCKS = SHARE // LANES
RIGHT_ROW = 2 * BLOCKS
LEFT_ROW = RIGHT_ROW + 2
PLAN_ROW = LEFT_ROW + 2
WINDOW = 40
WIDE = BLOCKS + 2
PANEL = 64
CHUNK = 256
HALF = COLS // 2
QUARTER = COLS // 4
PIECES = 3
EXACT = lax.Precision.HIGHEST


def params(mib=40):
    return pltpu.CompilerParams(vmem_limit_bytes=mib * 1024 * 1024)


def edges_kernel(state_hbm, resist_hbm, out_ref, ends, resist, sems):
    rows = 2 * PART // LANES
    loads = [
        pltpu.make_async_copy(resist_hbm, resist, sems.at[0]),
        pltpu.make_async_copy(state_hbm.at[pl.ds(0, 8), :], ends.at[0], sems.at[1]),
        pltpu.make_async_copy(state_hbm.at[pl.ds(rows - 8, 8), :], ends.at[1], sems.at[2]),
    ]
    for copy in loads:
        copy.start()
    for copy in loads:
        copy.wait()
    lane = lax.broadcasted_iota(jnp.int32, (1, LANES), 1)
    is_first, is_final = lane < HALO, lane >= LANES - HALO
    total = jnp.sum(jnp.sum(resist[...], axis=0, keepdims=True), axis=1, keepdims=True)
    outer = jnp.where(is_first, resist[0:1, :], jnp.where(is_final, resist[LANES - 1 : LANES, :], 0.0))
    upto = outer
    for step in (1, 2, 4, 8):
        upto = upto + jnp.where(lane >= step, pltpu.roll(upto, step, 1), 0.0)
    back = jnp.where(lane == LANES - 1, total, upto - upto[:, LANES - 1 : LANES])
    firsts = (ends[0, 0:1, :], ends[0, 1:2, :], resist[0:1, :], upto)
    finals = (ends[1, 6:7, :], ends[1, 7:8, :], resist[LANES - 1 : LANES, :], back)
    row = jnp.zeros((1, LANES), jnp.float32)
    for place, (first, final) in enumerate(zip(firsts, finals)):
        low, high = jnp.where(is_first, first, 0.0), jnp.where(is_final, final, 0.0)
        if place:
            low, high = pltpu.roll(low, place * HALO, 1), pltpu.roll(high, LANES - place * HALO, 1)
        row = row + low + high
    out_ref[...] = jnp.broadcast_to(row[None], (REACHES, 1, LANES))


def last_of(row, place):
    lane = lax.broadcasted_iota(jnp.int32, (1, LANES), 1)
    moved = pltpu.roll(row, place * HALO, 1) if place else row
    return jnp.where(lane >= LANES - HALO, moved, 0.0)


def first_of(row, place):
    lane = lax.broadcasted_iota(jnp.int32, (1, LANES), 1)
    moved = pltpu.roll(row, LANES - place * HALO, 1) if place else row
    return jnp.where(lane < HALO, moved, 0.0)


def window_kernel(state_ref, resist_ref, plan_ref, out_ref, aux_ref):
    rows = 2 * BLOCKS
    none = jnp.zeros((2, LANES), jnp.float32)
    for which in range(SCENS):
        start = which * rows
        out_ref[which, 0:rows, :] = state_ref[start : start + rows, :]
        after = state_ref[start + rows : start + rows + 2, :] if which < SCENS - 1 else none
        out_ref[which, RIGHT_ROW : RIGHT_ROW + 2, :] = after
        out_ref[which, LEFT_ROW : LEFT_ROW + 2, :] = state_ref[start - 2 : start, :] if which > 0 else none
        out_ref[which, PLAN_ROW:WINDOW, :] = jnp.zeros((WINDOW - PLAN_ROW, LANES), jnp.float32)
        out_ref[which, PLAN_ROW : PLAN_ROW + 1, 0 : 2 * STEPS + 1] = plan_ref[...]

    scen = lax.axis_index("scen")
    first = scen * BLOCKS
    row_left = resist_ref[pl.ds(jnp.maximum(first - 1, 0), 1), :]
    row_right = resist_ref[pl.ds(jnp.minimum(first + BLOCKS, LANES - 1), 1), :]
    mine = resist_ref[pl.ds(pl.multiple_of(first, BLOCKS), BLOCKS), :]
    spread = jnp.concatenate([mine, row_right, row_left, jnp.zeros((6, LANES), jnp.float32)], axis=0)
    row_id = lax.broadcasted_iota(jnp.int32, (LANES, 1), 0)
    before = jnp.sum(jnp.where(row_id < first, resist_ref[...], 0.0), axis=0, keepdims=True)
    base = jnp.sum(before, axis=1, keepdims=True)
    a = lax.broadcasted_iota(jnp.int32, (LANES, LANES), 0)
    b = lax.broadcasted_iota(jnp.int32, (LANES, LANES), 1)
    upto = jnp.where(a <= b, 1.0, 0.0).astype(jnp.float32)
    inside = jnp.dot(spread, upto, precision=EXACT, preferred_element_type=jnp.float32)
    totals = jnp.sum(spread, axis=1, keepdims=True)
    c = lax.broadcasted_iota(jnp.int32, (24, 24), 0)
    d = lax.broadcasted_iota(jnp.int32, (24, 24), 1)
    ahead = jnp.where((d < c) & (c <= BLOCKS) & (d < BLOCKS), 1.0, 0.0)
    ahead = ahead - jnp.where((c == BLOCKS + 1) & (d == BLOCKS + 1), 1.0, 0.0)
    shift = jnp.dot(
        ahead.astype(jnp.float32),
        jnp.broadcast_to(totals, (24, LANES)),
        precision=EXACT,
        preferred_element_type=jnp.float32,
    )
    aux_ref[0:24, :] = spread
    aux_ref[24:48, :] = base + (shift + inside)


def patch_kernel(win_ref, edge_ref, out_ref):
    reach = lax.axis_index("reach")
    previous = edge_ref[jnp.maximum(reach - 1, 0)]
    following = edge_ref[jnp.minimum(reach + 1, REACHES - 1)]
    for field in range(2):
        out_ref[0, LEFT_ROW + field : LEFT_ROW + field + 1, :] = last_of(previous, field)
        out_ref[SCENS - 1, RIGHT_ROW + field : RIGHT_ROW + field + 1, :] = first_of(following, field)


def step_kernel(win_ref, edge_ref, aux_ref, cols_ref, gram_ref, wide_ref, plan_ref, kept_ref, order_ref):
    scen = lax.axis_index("scen")
    reach = lax.axis_index("reach")
    lane = lax.broadcasted_iota(jnp.int32, (SCENS, LANES), 1)
    at_first = (lane == 0) & (scen == 0) & (reach == 0)
    at_last = (lane == LANES - 1) & (scen == SCENS - 1) & (reach == REACHES - 1)
    is_low = lane == 0
    is_high = lane == LANES - 1

    def taken(row):
        return win_ref[pl.ds(row, SCENS, stride=WINDOW), :]

    plans = taken(PLAN_ROW)
    head_plan, valve_plan = plans[:, 0:STEPS], plans[:, STEPS : 2 * STEPS]
    orifice = 1.0 / (1.0 + valve_plan)
    opened = valve_plan * orifice
    for moment in range(STEPS):
        for which, plan in enumerate((head_plan, orifice, opened)):
            plan_ref[which, moment * SCENS : (moment + 1) * SCENS, :] = jnp.broadcast_to(
                plan[:, moment : moment + 1], (SCENS, LANES)
            )
    steady = jnp.broadcast_to(plans[:, 2 * STEPS : 2 * STEPS + 1], (SCENS, LANES))
    scale = steady * jnp.abs(steady) * (1.0 / CELLS)
    mean_flow = steady * CELLS ** (-0.5)
    first_head = plan_ref[0, 0:SCENS, :]
    place = lax.broadcasted_iota(jnp.int32, (REACHES, 1, LANES), 0)
    held = edge_ref[...]
    at_total = slice(LANES - 3 * HALO - 1, LANES - 3 * HALO)
    upstream = jnp.sum(jnp.where(place < reach, held, 0.0), axis=0)[:, at_total]
    through = jnp.sum(jnp.where(place <= reach, held, 0.0), axis=0)[:, at_total]
    previous = edge_ref[jnp.maximum(reach - 1, 0)]
    following = edge_ref[jnp.minimum(reach + 1, REACHES - 1)]
    none = jnp.zeros((SCENS, LANES), jnp.float32)
    for j in range(WIDE):
        row = [LEFT_ROW, RIGHT_ROW][j > BLOCKS] if j in (0, WIDE - 1) else 2 * (j - 1)
        at = [BLOCKS + 1, BLOCKS][j > BLOCKS] if j in (0, WIDE - 1) else j - 1
        resist = aux_ref[at : at + 1, :]
        running = upstream + aux_ref[24 + at : 25 + at, :]
        head, flow = taken(row), taken(row + 1)
        if j in (0, WIDE - 1):
            if j == 0:
                beyond, base = scen == 0, upstream
                edge, upto = last_of(previous, 2), last_of(previous, 3)
                upto = jnp.where(is_high[0:1], 0.0, upto)
            else:
                beyond, base = scen == SCENS - 1, through
                edge, upto = first_of(following, 2), first_of(following, 3)
            resist = jnp.where(beyond, edge, resist)
            running = jnp.where(beyond, base + upto, running)
        wide_ref[0, j] = first_head - running * scale + head
        wide_ref[1, j] = mean_flow + flow
        for state in range(4):
            wide_ref[2 + state, j] = none
        wide_ref[6, j] = jnp.broadcast_to(resist, (SCENS, LANES))

    def two_steps(pair, carry):
        for half in range(2):
            plan_rows = pl.ds(pl.multiple_of((2 * pair + half) * SCENS, SCENS), SCENS)
            head_left = plan_ref[0, plan_rows, :]
            small = plan_ref[1, plan_rows, :]
            large = plan_ref[2, plan_rows, :]

            def sent(j):
                head, flow = wide_ref[0, j], wide_ref[1, j]
                friction = wide_ref[6, j] * flow * jnp.abs(flow) + (
                    (wide_ref[2, j] + wide_ref[3, j]) + (wide_ref[4, j] + wide_ref[5, j])
                )
                net = flow - friction
                return pltpu.roll(head + net, 1, 1), pltpu.roll(head - net, LANES - 1, 1)

            forward_before, (forward, backward) = None, sent(0)
            for j in range(WIDE):
                forward_after, backward_after = sent(j + 1) if j + 1 < WIDE else (forward, backward)
                if forward_before is None:
                    forward_before = forward
                from_left = jnp.where(is_low, forward_before, forward)
                from_right = jnp.where(is_high, backward_after, backward)
                new_head = 0.5 * (from_left + from_right)
                new_flow = 0.5 * (from_left - from_right)
                if j == 1:
                    new_head = jnp.where(at_first, head_left, new_head)
                    new_flow = jnp.where(at_first, head_left - from_right, new_flow)
                if j == BLOCKS:
                    new_head = jnp.where(at_last, from_left * small, new_head)
                    new_flow = jnp.where(at_last, from_left * large, new_flow)
                change = new_flow - wide_ref[1, j]
                wide_ref[0, j] = new_head
                wide_ref[1, j] = new_flow
                for state in range(4):
                    wide_ref[2 + state, j] = RETAINS[state] * wide_ref[2 + state, j] + SHARES[state] * change
                if 1 <= j <= BLOCKS:
                    for field, value in enumerate((new_head, new_flow)):
                        if half == 0:
                            kept_ref[field, j - 1] = value
                        else:
                            both = jnp.concatenate([kept_ref[field, j - 1], value], axis=0)
                            cols_ref[
                                field,
                                pl.ds(pl.multiple_of(pair * 2 * SCENS, 2 * SCENS), 2 * SCENS),
                                (j - 1) * LANES : j * LANES,
                            ] = both.astype(jnp.bfloat16)
                forward_before, forward, backward = forward, forward_after, backward_after
        return carry

    lax.fori_loop(0, STEPS // 2, two_steps, 0)

    total = None
    for field in range(2):
        columns = cols_ref[field]
        part = lax.dot_general(columns, columns, (((1,), (1,)), ((), ())), preferred_element_type=jnp.float32)
        total = part if total is None else total + part
    order_ref[...] = total
    rows = [order_ref[pl.ds(which, STEPS, stride=SCENS), :] for which in range(SCENS)]
    order_ref[...] = jnp.concatenate(rows, axis=0).T
    rows = [order_ref[pl.ds(which, STEPS, stride=SCENS), :] for which in range(SCENS)]
    high = lax.broadcasted_iota(jnp.int32, (QUARTER, COLS), 1) >= HALF
    upper, lower = jnp.concatenate(rows[4:6], axis=0), jnp.concatenate(rows[6:8], axis=0)
    packed = jnp.concatenate(rows[0:4] + [jnp.where(high, upper, pltpu.roll(lower, HALF, 1))], axis=0)
    for which in range(SCENS):
        for part in range(PIECES):
            at = (which * PIECES + part) * 4
            gram_ref[which, part] = packed[at : at + 4, :]


def fold_kernel(in_ref, out_ref):
    count, copies = in_ref.shape[0], out_ref.shape[0]
    total = in_ref[0]
    for which in range(1, count):
        total = total + in_ref[which]
    for which in range(copies):
        out_ref[which] = total


def basis_kernel(gram_ref, cols_ref, rows_ref, tri_ref, work_ref, turned_ref, order_ref, out_ref, sems):
    scale = 1.0 / (2 * CELLS)
    sub = lax.broadcasted_iota(jnp.int32, (8, COLS), 0)
    lane = lax.broadcasted_iota(jnp.int32, (8, COLS), 1)
    groups = PANEL // 8
    for field in range(2):
        for part in range(SHARE // CHUNK):
            turned_ref[field * (SHARE // CHUNK) + part] = cols_ref[field, :, part * CHUNK : (part + 1) * CHUNK].T
    for which in range(SCENS):
        for part in range(PIECES):
            at = (which * PIECES + part) * 4
            work_ref[at : at + 4, 0:COLS] = gram_ref[which, part] * scale
    work_ref[HALF + QUARTER :, 0:COLS] = pltpu.roll(work_ref[HALF : HALF + QUARTER, 0:COLS], HALF, 1)
    for g in range(COLS // 8):
        work_ref[8 * g : 8 * g + 8, COLS:] = jnp.where(lane == sub + 8 * g, 1.0, 0.0).astype(jnp.float32)
    inverse_rows = []
    for low in range(0, COLS, PANEL):
        left = [work_ref[low + 8 * g : low + 8 * g + 8, 0:COLS] for g in range(groups)]
        right = [work_ref[low + 8 * g : low + 8 * g + 8, COLS:] for g in range(groups)]
        scaled = []
        for own in range(groups):
            start = low + 8 * own
            wide = {
                g: [jnp.broadcast_to(left[g][:, start + j : start + j + 1], (8, COLS)) for j in range(8)]
                for g in range(own, groups)
            }
            inverses = jnp.zeros((8, COLS), jnp.float32)
            for k in range(8):
                inverse = 1.0 / wide[own][k][k : k + 1, :]
                inverses = jnp.where(sub == k, inverse, inverses)
                ahead = {j: wide[own][j][k : k + 1, :] * inverse for j in range(k + 1, 8)}
                row_left = left[own][k : k + 1, :] * inverse
                row_right = right[own][k : k + 1, :] * inverse
                for g in range(own, groups):
                    factor = wide[g][k]
                    if g == own:
                        factor = jnp.where(sub > k, factor, 0.0)
                    for j in ahead:
                        wide[g][j] = wide[g][j] - factor * ahead[j]
                    left[g] = left[g] - factor * row_left
                    right[g] = right[g] - factor * row_right
            scaled.append(left[own] * inverses)
            root = jnp.sqrt(inverses)
            tri_ref[start : start + 8, :] = jnp.where(lane >= sub + start, left[own] * root, 0.0)
            inverse_rows.append(right[own] * root)
        if low + PANEL < COLS:
            update = lax.dot_general(
                jnp.concatenate(scaled, axis=0),
                jnp.concatenate([jnp.concatenate(left, axis=0), jnp.concatenate(right, axis=0)], axis=1),
                (((0,), (0,)), ((), ())),
                precision=EXACT,
                preferred_element_type=jnp.float32,
            )
            work_ref[low + PANEL :, :] = work_ref[low + PANEL :, :] - update[low + PANEL :, :]
    order_ref[...] = jnp.concatenate(inverse_rows, axis=0).T
    inverse = jnp.concatenate([order_ref[pl.ds(n, SCENS, stride=STEPS), :] for n in range(STEPS)], axis=0)
    high = inverse.astype(jnp.bfloat16)
    rest = inverse - high.astype(jnp.float32)
    middle = rest.astype(jnp.bfloat16)
    both = jnp.concatenate([high, middle], axis=0)
    copies = []
    for field in range(2):
        for part in range(SHARE // CHUNK):
            slot = len(copies)
            piece = turned_ref[slot]
            out_ref[slot] = jnp.dot(
                jnp.concatenate([piece, piece], axis=1), both, preferred_element_type=jnp.float32
            )
            copy = pltpu.make_async_copy(
                out_ref.at[slot], rows_ref.at[field, pl.ds(part * CHUNK, CHUNK), :], sems.at[slot]
            )
            copy.start()
            copies.append(copy)
    for copy in copies:
        copy.wait()


def fold(value, copies):
    return pl.pallas_call(
        fold_kernel,
        out_shape=jax.ShapeDtypeStruct((copies,) + value.shape[1:], jnp.float32),
        compiler_params=params(),
    )(value)


def exchanged(value, axis, groups=None):
    return lax.all_to_all(value, axis, split_axis=0, concat_axis=0, axis_index_groups=groups, tiled=True)


def local(perturb, resist, flow_rate, head_plan, valve_plan):
    f32 = jnp.float32
    vmem = pl.BlockSpec(memory_space=pltpu.VMEM)
    hbm = pl.BlockSpec(memory_space=pltpu.HBM)
    blocks = PART // LANES
    state = perturb.reshape(2, blocks, LANES).transpose(1, 0, 2).reshape(2 * blocks, LANES)
    resist = resist.reshape(LANES, LANES)
    edges = pl.pallas_call(
        edges_kernel,
        in_specs=[hbm, hbm],
        out_specs=vmem,
        out_shape=jax.ShapeDtypeStruct((REACHES, 1, LANES), f32),
        scratch_shapes=[
            pltpu.VMEM((2, 8, LANES), f32),
            pltpu.VMEM((LANES, LANES), f32),
            pltpu.SemaphoreType.DMA((3,)),
        ],
        compiler_params=params(61),
    )(state, resist)
    edges = exchanged(edges, "reach")
    plans = jnp.concatenate([head_plan, valve_plan, flow_rate.reshape(1, 1)], axis=1)
    windows, aux = pl.pallas_call(
        window_kernel,
        in_specs=[vmem, vmem, vmem],
        out_shape=(
            jax.ShapeDtypeStruct((SCENS, WINDOW, LANES), f32),
            jax.ShapeDtypeStruct((48, LANES), f32),
        ),
        compiler_params=params(),
    )(state, resist, plans)
    windows = pl.pallas_call(
        patch_kernel,
        in_specs=[vmem, vmem],
        out_specs=vmem,
        out_shape=jax.ShapeDtypeStruct((SCENS, WINDOW, LANES), f32),
        input_output_aliases={0: 0},
        compiler_params=params(),
    )(windows, edges)
    windows = exchanged(windows, "scen").reshape(SCENS * WINDOW, LANES)
    columns, gram = pl.pallas_call(
        step_kernel,
        out_shape=(
            jax.ShapeDtypeStruct((2, COLS, SHARE), jnp.bfloat16),
            jax.ShapeDtypeStruct((SCENS, PIECES, 4, COLS), f32),
        ),
        scratch_shapes=[
            pltpu.VMEM((7, WIDE, SCENS, LANES), f32),
            pltpu.VMEM((3, STEPS * SCENS, LANES), f32),
            pltpu.VMEM((2, BLOCKS, SCENS, LANES), f32),
            pltpu.VMEM((COLS, COLS), f32),
        ],
        compiler_params=params(),
    )(windows, edges, aux)
    along = [[RING * a + b for b in range(RING)] for a in range(RING)]
    across = [[RING * b + a for b in range(RING)] for a in range(RING)]
    gram = fold(exchanged(gram, "scen"), RING)
    gram = fold(exchanged(gram, "reach", along), RING)
    gram = fold(exchanged(gram, "reach", across), SCENS)
    gram = exchanged(gram, "scen")
    chunks = 2 * SHARE // CHUNK
    return pl.pallas_call(
        basis_kernel,
        in_specs=[vmem, vmem],
        out_specs=(pl.BlockSpec(memory_space=pl.ANY), vmem),
        out_shape=(
            jax.ShapeDtypeStruct((2, SHARE, COLS), f32),
            jax.ShapeDtypeStruct((COLS, COLS), f32),
        ),
        scratch_shapes=[
            pltpu.VMEM((COLS, 2 * COLS), f32),
            pltpu.VMEM((chunks, CHUNK, COLS), jnp.bfloat16),
            pltpu.VMEM((COLS, COLS), f32),
            pltpu.VMEM((chunks, CHUNK, COLS), f32),
            pltpu.SemaphoreType.DMA((chunks,)),
        ],
        compiler_params=params(),
    )(gram, columns)


def solution(mesh):
    in_specs = (P("scen", None, "reach"), P("reach"), P("scen"), P("scen", None), P("scen", None))
    out_specs = (P(None, ("reach", "scen"), None), P())
    return jax.shard_map(local, mesh=mesh, in_specs=in_specs, out_specs=out_specs, check_vma=False)
```

```python
import jax
import jax.numpy as jnp
from jax import lax
from jax.experimental import pallas as pl
from jax.experimental.pallas import tpu as pltpu
from jax.sharding import PartitionSpec as P

STEPS = 16
SHARES = (0.06, 0.04, 0.025, 0.015)
RETAINS = (0.2, 0.5, 0.8, 0.95)
LANES = 128
HALO = 16
SCENS = 8
REACHES = 64
RING = 8
COLS = SCENS * STEPS
CELLS = 1048576
PART = CELLS // REACHES
SHARE = PART // SCENS
BLOCKS = SHARE // LANES
RIGHT_ROW = 2 * BLOCKS
LEFT_ROW = RIGHT_ROW + 2
PLAN_ROW = LEFT_ROW + 2
WINDOW = 40
WIDE = BLOCKS + 1
PANEL = 64
CHUNK = 256
HALF = COLS // 2
QUARTER = COLS // 4
PIECES = 3
EXACT = lax.Precision.HIGHEST


def params(mib=40):
    return pltpu.CompilerParams(vmem_limit_bytes=mib * 1024 * 1024)


def edges_kernel(state_hbm, resist_hbm, out_ref, ends, resist, sems):
    rows = 2 * PART // LANES
    loads = [
        pltpu.make_async_copy(resist_hbm, resist, sems.at[0]),
        pltpu.make_async_copy(state_hbm.at[pl.ds(0, 8), :], ends.at[0], sems.at[1]),
        pltpu.make_async_copy(state_hbm.at[pl.ds(rows - 8, 8), :], ends.at[1], sems.at[2]),
    ]
    for copy in loads:
        copy.start()
    for copy in loads:
        copy.wait()
    lane = lax.broadcasted_iota(jnp.int32, (1, LANES), 1)
    is_first, is_final = lane < HALO, lane >= LANES - HALO
    total = jnp.sum(jnp.sum(resist[...], axis=0, keepdims=True), axis=1, keepdims=True)
    firsts = [jnp.where(is_first, row, 0.0) for row in (ends[0, 0:1, :], ends[0, 1:2, :], resist[0:1, :])]
    finals = [
        jnp.where(is_final, row, 0.0) for row in (ends[1, 6:7, :], ends[1, 7:8, :], resist[LANES - 1 : LANES, :])
    ]

    def moved(row, by):
        return pltpu.roll(row, by % LANES, 1) if by % LANES else row

    row = firsts[0] + finals[0]
    for place in (1, 2):
        row = row + moved(firsts[place], place * HALO) + moved(finals[place], -place * HALO)
    ahead, behind = firsts[2], moved(finals[2], -1)
    for step in (1, 2, 3):
        ahead = ahead + moved(firsts[2], step)
        behind = behind + moved(finals[2], -1 - step)
    at = 3 * HALO
    upto, rest = moved(ahead, at), moved(behind, -at)
    for step in (4, 8, 12):
        upto = upto + moved(ahead, at + step)
        rest = rest + moved(behind, -at - step)
    row = jnp.where((lane >= at) & (lane < at + HALO), upto, row)
    row = jnp.where((lane >= LANES - at - HALO) & (lane < LANES - at), -rest, row)
    row = jnp.where(lane == LANES - at - 1, total, row)
    out_ref[...] = jnp.broadcast_to(row[None], (REACHES, 1, LANES))


def last_of(row, place):
    lane = lax.broadcasted_iota(jnp.int32, (1, LANES), 1)
    moved = pltpu.roll(row, place * HALO, 1) if place else row
    return jnp.where(lane >= LANES - HALO, moved, 0.0)


def first_of(row, place):
    lane = lax.broadcasted_iota(jnp.int32, (1, LANES), 1)
    moved = pltpu.roll(row, LANES - place * HALO, 1) if place else row
    return jnp.where(lane < HALO, moved, 0.0)


def window_kernel(state_ref, resist_ref, plan_ref, out_ref, aux_ref):
    rows = 2 * BLOCKS
    none = jnp.zeros((2, LANES), jnp.float32)
    for which in range(SCENS):
        start = which * rows
        out_ref[which, 0:rows, :] = state_ref[start : start + rows, :]
        after = state_ref[start + rows : start + rows + 2, :] if which < SCENS - 1 else none
        out_ref[which, RIGHT_ROW : RIGHT_ROW + 2, :] = after
        out_ref[which, LEFT_ROW : LEFT_ROW + 2, :] = state_ref[start - 2 : start, :] if which > 0 else none
        out_ref[which, PLAN_ROW:WINDOW, :] = jnp.zeros((WINDOW - PLAN_ROW, LANES), jnp.float32)
        out_ref[which, PLAN_ROW : PLAN_ROW + 1, 0 : 2 * STEPS + 1] = plan_ref[...]

    scen = lax.axis_index("scen")
    first = scen * BLOCKS
    row_left = resist_ref[pl.ds(jnp.maximum(first - 1, 0), 1), :]
    row_right = resist_ref[pl.ds(jnp.minimum(first + BLOCKS, LANES - 1), 1), :]
    mine = resist_ref[pl.ds(pl.multiple_of(first, BLOCKS), BLOCKS), :]
    spread = jnp.concatenate([mine, row_right, row_left, jnp.zeros((6, LANES), jnp.float32)], axis=0)
    row_id = lax.broadcasted_iota(jnp.int32, (LANES, 1), 0)
    before = jnp.sum(jnp.where(row_id < first, resist_ref[...], 0.0), axis=0, keepdims=True)
    base = jnp.sum(before, axis=1, keepdims=True)
    a = lax.broadcasted_iota(jnp.int32, (LANES, LANES), 0)
    b = lax.broadcasted_iota(jnp.int32, (LANES, LANES), 1)
    upto = jnp.where(a <= b, 1.0, 0.0).astype(jnp.float32)
    inside = jnp.dot(spread, upto, precision=EXACT, preferred_element_type=jnp.float32)
    totals = jnp.sum(spread, axis=1, keepdims=True)
    c = lax.broadcasted_iota(jnp.int32, (24, 24), 0)
    d = lax.broadcasted_iota(jnp.int32, (24, 24), 1)
    ahead = jnp.where((d < c) & (c <= BLOCKS) & (d < BLOCKS), 1.0, 0.0)
    ahead = ahead - jnp.where((c == BLOCKS + 1) & (d == BLOCKS + 1), 1.0, 0.0)
    shift = jnp.dot(
        ahead.astype(jnp.float32),
        jnp.broadcast_to(totals, (24, LANES)),
        precision=EXACT,
        preferred_element_type=jnp.float32,
    )
    aux_ref[0:24, :] = spread
    aux_ref[24:48, :] = base + (shift + inside)


def patch_kernel(win_ref, edge_ref, out_ref):
    reach = lax.axis_index("reach")
    previous = edge_ref[jnp.maximum(reach - 1, 0)]
    following = edge_ref[jnp.minimum(reach + 1, REACHES - 1)]
    for field in range(2):
        out_ref[0, LEFT_ROW + field : LEFT_ROW + field + 1, :] = last_of(previous, field)
        out_ref[SCENS - 1, RIGHT_ROW + field : RIGHT_ROW + field + 1, :] = first_of(following, field)


def step_kernel(win_ref, edge_ref, aux_ref, cols_ref, gram_ref, wide_ref, plan_ref, kept_ref, order_ref):
    scen = lax.axis_index("scen")
    reach = lax.axis_index("reach")
    lane = lax.broadcasted_iota(jnp.int32, (SCENS, LANES), 1)
    at_first = (lane == 0) & (scen == 0) & (reach == 0)
    at_last = (lane == LANES - 1) & (scen == SCENS - 1) & (reach == REACHES - 1)
    is_low = lane == 0
    is_high = lane == LANES - 1

    def taken(row):
        return win_ref[pl.ds(row, SCENS, stride=WINDOW), :]

    plans = taken(PLAN_ROW)
    head_plan, valve_plan = plans[:, 0:STEPS], plans[:, STEPS : 2 * STEPS]
    orifice = 1.0 / (1.0 + valve_plan)
    opened = valve_plan * orifice
    for moment in range(STEPS):
        for which, plan in enumerate((head_plan, orifice, opened)):
            plan_ref[which, moment * SCENS : (moment + 1) * SCENS, :] = jnp.broadcast_to(
                plan[:, moment : moment + 1], (SCENS, LANES)
            )
    steady = jnp.broadcast_to(plans[:, 2 * STEPS : 2 * STEPS + 1], (SCENS, LANES))
    scale = steady * jnp.abs(steady) * (1.0 / CELLS)
    mean_flow = steady * CELLS ** (-0.5)
    first_head = plan_ref[0, 0:SCENS, :]
    place = lax.broadcasted_iota(jnp.int32, (REACHES, 1, LANES), 0)
    held = edge_ref[...]
    at_total = slice(LANES - 3 * HALO - 1, LANES - 3 * HALO)
    upstream = jnp.sum(jnp.where(place < reach, held, 0.0), axis=0)[:, at_total]
    through = jnp.sum(jnp.where(place <= reach, held, 0.0), axis=0)[:, at_total]
    previous = edge_ref[jnp.maximum(reach - 1, 0)]
    following = edge_ref[jnp.minimum(reach + 1, REACHES - 1)]
    none = jnp.zeros((SCENS, LANES), jnp.float32)
    is_left = lane >= LANES // 2

    def outer(row, at, beyond, base, edge, upto):
        resist = jnp.where(beyond, edge, aux_ref[at : at + 1, :])
        running = jnp.where(beyond, base + upto, upstream + aux_ref[24 + at : 25 + at, :])
        return taken(row), taken(row + 1), resist, running

    before = jnp.where(is_high[0:1], 0.0, last_of(previous, 3))
    left = outer(LEFT_ROW, BLOCKS + 1, scen == 0, upstream, last_of(previous, 2), before)
    right = outer(
        RIGHT_ROW, BLOCKS, scen == SCENS - 1, through, first_of(following, 2), first_of(following, 3)
    )
    for j in range(WIDE):
        if j == 0:
            head, flow, resist, running = (jnp.where(is_left, a, b) for a, b in zip(left, right))
        else:
            head, flow = taken(2 * (j - 1)), taken(2 * (j - 1) + 1)
            resist = aux_ref[j - 1 : j, :]
            running = upstream + aux_ref[23 + j : 24 + j, :]
        wide_ref[0, j] = first_head - running * scale + head
        wide_ref[1, j] = mean_flow + flow
        for state in range(4):
            wide_ref[2 + state, j] = none
        wide_ref[6, j] = jnp.broadcast_to(resist, (SCENS, LANES))

    def two_steps(pair, carry):
        for half in range(2):
            plan_rows = pl.ds(pl.multiple_of((2 * pair + half) * SCENS, SCENS), SCENS)
            head_left = plan_ref[0, plan_rows, :]
            small = plan_ref[1, plan_rows, :]
            large = plan_ref[2, plan_rows, :]

            def sent(j):
                head, flow = wide_ref[0, j], wide_ref[1, j]
                friction = wide_ref[6, j] * flow * jnp.abs(flow) + (
                    (wide_ref[2, j] + wide_ref[3, j]) + (wide_ref[4, j] + wide_ref[5, j])
                )
                net = flow - friction
                return pltpu.roll(head + net, 1, 1), pltpu.roll(head - net, LANES - 1, 1)

            ring_start, ring_end = sent(0), sent(WIDE - 1)
            forward_before, (forward, backward) = ring_end[0], ring_start
            for j in range(WIDE):
                forward_after, backward_after = {WIDE - 2: ring_end, WIDE - 1: ring_start}.get(j) or sent(j + 1)
                from_left = jnp.where(is_low, forward_before, forward)
                from_right = jnp.where(is_high, backward_after, backward)
                new_head = 0.5 * (from_left + from_right)
                new_flow = 0.5 * (from_left - from_right)
                if j == 1:
                    new_head = jnp.where(at_first, head_left, new_head)
                    new_flow = jnp.where(at_first, head_left - from_right, new_flow)
                if j == BLOCKS:
                    new_head = jnp.where(at_last, from_left * small, new_head)
                    new_flow = jnp.where(at_last, from_left * large, new_flow)
                change = new_flow - wide_ref[1, j]
                wide_ref[0, j] = new_head
                wide_ref[1, j] = new_flow
                for state in range(4):
                    wide_ref[2 + state, j] = RETAINS[state] * wide_ref[2 + state, j] + SHARES[state] * change
                if 1 <= j <= BLOCKS:
                    for field, value in enumerate((new_head, new_flow)):
                        if half == 0:
                            kept_ref[field, j - 1] = value
                        else:
                            both = jnp.concatenate([kept_ref[field, j - 1], value], axis=0)
                            cols_ref[
                                field,
                                pl.ds(pl.multiple_of(pair * 2 * SCENS, 2 * SCENS), 2 * SCENS),
                                (j - 1) * LANES : j * LANES,
                            ] = both.astype(jnp.bfloat16)
                forward_before, forward, backward = forward, forward_after, backward_after
        return carry

    lax.fori_loop(0, STEPS // 2, two_steps, 0)

    total = None
    for field in range(2):
        columns = cols_ref[field]
        part = lax.dot_general(columns, columns, (((1,), (1,)), ((), ())), preferred_element_type=jnp.float32)
        total = part if total is None else total + part
    order_ref[...] = total
    rows = [order_ref[pl.ds(which, STEPS, stride=SCENS), :] for which in range(SCENS)]
    order_ref[...] = jnp.concatenate(rows, axis=0).T
    rows = [order_ref[pl.ds(which, STEPS, stride=SCENS), :] for which in range(SCENS)]
    high = lax.broadcasted_iota(jnp.int32, (QUARTER, COLS), 1) >= HALF
    upper, lower = jnp.concatenate(rows[4:6], axis=0), jnp.concatenate(rows[6:8], axis=0)
    packed = jnp.concatenate(rows[0:4] + [jnp.where(high, upper, pltpu.roll(lower, HALF, 1))], axis=0)
    for which in range(SCENS):
        for part in range(PIECES):
            at = (which * PIECES + part) * 4
            gram_ref[which, part] = packed[at : at + 4, :]


def fold_kernel(in_ref, out_ref):
    count, copies = in_ref.shape[0], out_ref.shape[0]
    total = in_ref[0]
    for which in range(1, count):
        total = total + in_ref[which]
    for which in range(copies):
        out_ref[which] = total


def basis_kernel(gram_ref, cols_ref, rows_ref, tri_ref, work_ref, turned_ref, order_ref, out_ref, sems):
    scale = 1.0 / (2 * CELLS)
    sub = lax.broadcasted_iota(jnp.int32, (8, COLS), 0)
    lane = lax.broadcasted_iota(jnp.int32, (8, COLS), 1)
    groups = PANEL // 8
    for field in range(2):
        for part in range(SHARE // CHUNK):
            turned_ref[field * (SHARE // CHUNK) + part] = cols_ref[field, :, part * CHUNK : (part + 1) * CHUNK].T
    for which in range(SCENS):
        for part in range(PIECES):
            at = (which * PIECES + part) * 4
            work_ref[at : at + 4, 0:COLS] = gram_ref[which, part] * scale
    work_ref[HALF + QUARTER :, 0:COLS] = pltpu.roll(work_ref[HALF : HALF + QUARTER, 0:COLS], HALF, 1)
    for g in range(COLS // 8):
        work_ref[8 * g : 8 * g + 8, COLS:] = jnp.where(lane == sub + 8 * g, 1.0, 0.0).astype(jnp.float32)
    inverse_rows = []
    for low in range(0, COLS, PANEL):
        left = [work_ref[low + 8 * g : low + 8 * g + 8, 0:COLS] for g in range(groups)]
        right = [work_ref[low + 8 * g : low + 8 * g + 8, COLS:] for g in range(groups)]
        scaled = []
        for own in range(groups):
            start = low + 8 * own
            wide = {
                g: [jnp.broadcast_to(left[g][:, start + j : start + j + 1], (8, COLS)) for j in range(8)]
                for g in range(own, groups)
            }
            inverses = jnp.zeros((8, COLS), jnp.float32)
            for k in range(8):
                inverse = 1.0 / wide[own][k][k : k + 1, :]
                inverses = jnp.where(sub == k, inverse, inverses)
                ahead = {j: wide[own][j][k : k + 1, :] * inverse for j in range(k + 1, 8)}
                row_left = left[own][k : k + 1, :] * inverse
                row_right = right[own][k : k + 1, :] * inverse
                for g in range(own, groups):
                    factor = wide[g][k]
                    if g == own:
                        factor = jnp.where(sub > k, factor, 0.0)
                    for j in ahead:
                        wide[g][j] = wide[g][j] - factor * ahead[j]
                    left[g] = left[g] - factor * row_left
                    right[g] = right[g] - factor * row_right
            scaled.append(left[own] * inverses)
            root = jnp.sqrt(inverses)
            tri_ref[start : start + 8, :] = jnp.where(lane >= sub + start, left[own] * root, 0.0)
            inverse_rows.append(right[own] * root)
        if low + PANEL < COLS:
            update = lax.dot_general(
                jnp.concatenate(scaled, axis=0),
                jnp.concatenate([jnp.concatenate(left, axis=0), jnp.concatenate(right, axis=0)], axis=1),
                (((0,), (0,)), ((), ())),
                precision=EXACT,
                preferred_element_type=jnp.float32,
            )
            work_ref[low + PANEL :, :] = work_ref[low + PANEL :, :] - update[low + PANEL :, :]
    order_ref[...] = jnp.concatenate(inverse_rows, axis=0).T
    inverse = jnp.concatenate([order_ref[pl.ds(n, SCENS, stride=STEPS), :] for n in range(STEPS)], axis=0)
    high = inverse.astype(jnp.bfloat16)
    rest = inverse - high.astype(jnp.float32)
    middle = rest.astype(jnp.bfloat16)
    both = jnp.concatenate([high, middle], axis=0)
    copies = []
    for field in range(2):
        for part in range(SHARE // CHUNK):
            slot = len(copies)
            piece = turned_ref[slot]
            out_ref[slot] = jnp.dot(
                jnp.concatenate([piece, piece], axis=1), both, preferred_element_type=jnp.float32
            )
            copy = pltpu.make_async_copy(
                out_ref.at[slot], rows_ref.at[field, pl.ds(part * CHUNK, CHUNK), :], sems.at[slot]
            )
            copy.start()
            copies.append(copy)
    for copy in copies:
        copy.wait()


def fold(value, copies):
    return pl.pallas_call(
        fold_kernel,
        out_shape=jax.ShapeDtypeStruct((copies,) + value.shape[1:], jnp.float32),
        compiler_params=params(),
    )(value)


def exchanged(value, axis, groups=None):
    return lax.all_to_all(value, axis, split_axis=0, concat_axis=0, axis_index_groups=groups, tiled=True)


def local(perturb, resist, flow_rate, head_plan, valve_plan):
    f32 = jnp.float32
    vmem = pl.BlockSpec(memory_space=pltpu.VMEM)
    hbm = pl.BlockSpec(memory_space=pltpu.HBM)
    blocks = PART // LANES
    state = perturb.reshape(2, blocks, LANES).transpose(1, 0, 2).reshape(2 * blocks, LANES)
    resist = resist.reshape(LANES, LANES)
    edges = pl.pallas_call(
        edges_kernel,
        in_specs=[hbm, hbm],
        out_specs=vmem,
        out_shape=jax.ShapeDtypeStruct((REACHES, 1, LANES), f32),
        scratch_shapes=[
            pltpu.VMEM((2, 8, LANES), f32),
            pltpu.VMEM((LANES, LANES), f32),
            pltpu.SemaphoreType.DMA((3,)),
        ],
        compiler_params=params(61),
    )(state, resist)
    edges = exchanged(edges, "reach")
    plans = jnp.concatenate([head_plan, valve_plan, flow_rate.reshape(1, 1)], axis=1)
    windows, aux = pl.pallas_call(
        window_kernel,
        in_specs=[vmem, vmem, vmem],
        out_shape=(
            jax.ShapeDtypeStruct((SCENS, WINDOW, LANES), f32),
            jax.ShapeDtypeStruct((48, LANES), f32),
        ),
        compiler_params=params(),
    )(state, resist, plans)
    windows = pl.pallas_call(
        patch_kernel,
        in_specs=[vmem, vmem],
        out_specs=vmem,
        out_shape=jax.ShapeDtypeStruct((SCENS, WINDOW, LANES), f32),
        input_output_aliases={0: 0},
        compiler_params=params(),
    )(windows, edges)
    windows = exchanged(windows, "scen").reshape(SCENS * WINDOW, LANES)
    columns, gram = pl.pallas_call(
        step_kernel,
        out_shape=(
            jax.ShapeDtypeStruct((2, COLS, SHARE), jnp.bfloat16),
            jax.ShapeDtypeStruct((SCENS, PIECES, 4, COLS), f32),
        ),
        scratch_shapes=[
            pltpu.VMEM((7, WIDE, SCENS, LANES), f32),
            pltpu.VMEM((3, STEPS * SCENS, LANES), f32),
            pltpu.VMEM((2, BLOCKS, SCENS, LANES), f32),
            pltpu.VMEM((COLS, COLS), f32),
        ],
        compiler_params=params(),
    )(windows, edges, aux)
    gram = fold(exchanged(gram, "scen"), REACHES)
    gram = fold(exchanged(gram, "reach"), SCENS)
    gram = exchanged(gram, "scen")
    chunks = 2 * SHARE // CHUNK
    return pl.pallas_call(
        basis_kernel,
        in_specs=[vmem, vmem],
        out_specs=(pl.BlockSpec(memory_space=pl.ANY), vmem),
        out_shape=(
            jax.ShapeDtypeStruct((2, SHARE, COLS), f32),
            jax.ShapeDtypeStruct((COLS, COLS), f32),
        ),
        scratch_shapes=[
            pltpu.VMEM((COLS, 2 * COLS), f32),
            pltpu.VMEM((chunks, CHUNK, COLS), jnp.bfloat16),
            pltpu.VMEM((COLS, COLS), f32),
            pltpu.VMEM((chunks, CHUNK, COLS), f32),
            pltpu.SemaphoreType.DMA((chunks,)),
        ],
        compiler_params=params(),
    )(gram, columns)


def solution(mesh):
    in_specs = (P("scen", None, "reach"), P("reach"), P("scen"), P("scen", None), P("scen", None))
    out_specs = (P(None, ("reach", "scen"), None), P())
    return jax.shard_map(local, mesh=mesh, in_specs=in_specs, out_specs=out_specs, check_vma=False)
```

```python
import jax
import jax.numpy as jnp
from jax import lax
from jax.experimental import pallas as pl
from jax.experimental.pallas import tpu as pltpu
from jax.sharding import PartitionSpec as P

STEPS = 16
SHARES = (0.06, 0.04, 0.025, 0.015)
RETAINS = (0.2, 0.5, 0.8, 0.95)
LANES = 128
HALO = 16
SCENS = 8
REACHES = 64
RING = 8
COLS = SCENS * STEPS
CELLS = 1048576
PART = CELLS // REACHES
SHARE = PART // SCENS
BLOCKS = SHARE // LANES
RIGHT_ROW = 2 * BLOCKS
LEFT_ROW = RIGHT_ROW + 2
PLAN_ROW = LEFT_ROW + 2
WINDOW = 40
WIDE = BLOCKS + 1
PANEL = 64
CHUNK = 256
HALF = COLS // 2
QUARTER = COLS // 4
PIECES = 5
EXACT = lax.Precision.HIGHEST


def params(mib=40):
    return pltpu.CompilerParams(vmem_limit_bytes=mib * 1024 * 1024)


def edges_kernel(state_hbm, resist_hbm, out_ref, ends, resist, sems):
    rows = 2 * PART // LANES
    loads = [
        pltpu.make_async_copy(resist_hbm, resist, sems.at[0]),
        pltpu.make_async_copy(state_hbm.at[pl.ds(0, 8), :], ends.at[0], sems.at[1]),
        pltpu.make_async_copy(state_hbm.at[pl.ds(rows - 8, 8), :], ends.at[1], sems.at[2]),
    ]
    for copy in loads:
        copy.start()
    for copy in loads:
        copy.wait()
    lane = lax.broadcasted_iota(jnp.int32, (1, LANES), 1)
    is_first, is_final = lane < HALO, lane >= LANES - HALO
    total = jnp.sum(jnp.sum(resist[...], axis=0, keepdims=True), axis=1, keepdims=True)
    firsts = [jnp.where(is_first, row, 0.0) for row in (ends[0, 0:1, :], ends[0, 1:2, :], resist[0:1, :])]
    finals = [
        jnp.where(is_final, row, 0.0) for row in (ends[1, 6:7, :], ends[1, 7:8, :], resist[LANES - 1 : LANES, :])
    ]

    def moved(row, by):
        return pltpu.roll(row, by % LANES, 1) if by % LANES else row

    row = firsts[0] + finals[0]
    for place in (1, 2):
        row = row + moved(firsts[place], place * HALO) + moved(finals[place], -place * HALO)
    ahead, behind = firsts[2], moved(finals[2], -1)
    for step in (1, 2, 3):
        ahead = ahead + moved(firsts[2], step)
        behind = behind + moved(finals[2], -1 - step)
    at = 3 * HALO
    upto, rest = moved(ahead, at), moved(behind, -at)
    for step in (4, 8, 12):
        upto = upto + moved(ahead, at + step)
        rest = rest + moved(behind, -at - step)
    row = jnp.where((lane >= at) & (lane < at + HALO), upto, row)
    row = jnp.where((lane >= LANES - at - HALO) & (lane < LANES - at), -rest, row)
    row = jnp.where(lane == LANES - at - 1, total, row)
    out_ref[...] = jnp.broadcast_to(row[None], (REACHES, 1, LANES))


def last_of(row, place):
    lane = lax.broadcasted_iota(jnp.int32, (1, LANES), 1)
    moved = pltpu.roll(row, place * HALO, 1) if place else row
    return jnp.where(lane >= LANES - HALO, moved, 0.0)


def first_of(row, place):
    lane = lax.broadcasted_iota(jnp.int32, (1, LANES), 1)
    moved = pltpu.roll(row, LANES - place * HALO, 1) if place else row
    return jnp.where(lane < HALO, moved, 0.0)


def window_kernel(state_ref, resist_ref, plan_ref, out_ref, aux_ref):
    rows = 2 * BLOCKS
    none = jnp.zeros((2, LANES), jnp.float32)
    for which in range(SCENS):
        start = which * rows
        out_ref[which, 0:rows, :] = state_ref[start : start + rows, :]
        after = state_ref[start + rows : start + rows + 2, :] if which < SCENS - 1 else none
        out_ref[which, RIGHT_ROW : RIGHT_ROW + 2, :] = after
        out_ref[which, LEFT_ROW : LEFT_ROW + 2, :] = state_ref[start - 2 : start, :] if which > 0 else none
        out_ref[which, PLAN_ROW:WINDOW, :] = jnp.zeros((WINDOW - PLAN_ROW, LANES), jnp.float32)
        out_ref[which, PLAN_ROW : PLAN_ROW + 1, 0 : 2 * STEPS + 1] = plan_ref[...]

    scen = lax.axis_index("scen")
    first = scen * BLOCKS
    row_left = resist_ref[pl.ds(jnp.maximum(first - 1, 0), 1), :]
    row_right = resist_ref[pl.ds(jnp.minimum(first + BLOCKS, LANES - 1), 1), :]
    mine = resist_ref[pl.ds(pl.multiple_of(first, BLOCKS), BLOCKS), :]
    spread = jnp.concatenate([mine, row_right, row_left, jnp.zeros((6, LANES), jnp.float32)], axis=0)
    row_id = lax.broadcasted_iota(jnp.int32, (LANES, 1), 0)
    before = jnp.sum(jnp.where(row_id < first, resist_ref[...], 0.0), axis=0, keepdims=True)
    base = jnp.sum(before, axis=1, keepdims=True)
    a = lax.broadcasted_iota(jnp.int32, (LANES, LANES), 0)
    b = lax.broadcasted_iota(jnp.int32, (LANES, LANES), 1)
    upto = jnp.where(a <= b, 1.0, 0.0).astype(jnp.float32)
    inside = jnp.dot(spread, upto, precision=EXACT, preferred_element_type=jnp.float32)
    totals = jnp.sum(spread, axis=1, keepdims=True)
    c = lax.broadcasted_iota(jnp.int32, (24, 24), 0)
    d = lax.broadcasted_iota(jnp.int32, (24, 24), 1)
    ahead = jnp.where((d < c) & (c <= BLOCKS) & (d < BLOCKS), 1.0, 0.0)
    ahead = ahead - jnp.where((c == BLOCKS + 1) & (d == BLOCKS + 1), 1.0, 0.0)
    shift = jnp.dot(
        ahead.astype(jnp.float32),
        jnp.broadcast_to(totals, (24, LANES)),
        precision=EXACT,
        preferred_element_type=jnp.float32,
    )
    aux_ref[0:24, :] = spread
    aux_ref[24:48, :] = base + (shift + inside)


def patch_kernel(win_ref, edge_ref, out_ref):
    reach = lax.axis_index("reach")
    previous = edge_ref[jnp.maximum(reach - 1, 0)]
    following = edge_ref[jnp.minimum(reach + 1, REACHES - 1)]
    for field in range(2):
        out_ref[0, LEFT_ROW + field : LEFT_ROW + field + 1, :] = last_of(previous, field)
        out_ref[SCENS - 1, RIGHT_ROW + field : RIGHT_ROW + field + 1, :] = first_of(following, field)


def step_kernel(win_ref, edge_ref, aux_ref, cols_ref, gram_ref, wide_ref, plan_ref, kept_ref, order_ref):
    scen = lax.axis_index("scen")
    reach = lax.axis_index("reach")
    lane = lax.broadcasted_iota(jnp.int32, (SCENS, LANES), 1)
    at_first = (lane == 0) & (scen == 0) & (reach == 0)
    at_last = (lane == LANES - 1) & (scen == SCENS - 1) & (reach == REACHES - 1)
    is_low = lane == 0
    is_high = lane == LANES - 1

    def taken(row):
        return win_ref[pl.ds(row, SCENS, stride=WINDOW), :]

    plans = taken(PLAN_ROW)
    head_plan, valve_plan = plans[:, 0:STEPS], plans[:, STEPS : 2 * STEPS]
    orifice = 1.0 / (1.0 + valve_plan)
    opened = valve_plan * orifice
    for moment in range(STEPS):
        for which, plan in enumerate((head_plan, orifice, opened)):
            plan_ref[which, moment * SCENS : (moment + 1) * SCENS, :] = jnp.broadcast_to(
                plan[:, moment : moment + 1], (SCENS, LANES)
            )
    steady = jnp.broadcast_to(plans[:, 2 * STEPS : 2 * STEPS + 1], (SCENS, LANES))
    scale = steady * jnp.abs(steady) * (1.0 / CELLS)
    mean_flow = steady * CELLS ** (-0.5)
    first_head = plan_ref[0, 0:SCENS, :]
    place = lax.broadcasted_iota(jnp.int32, (REACHES, 1, LANES), 0)
    held = edge_ref[...]
    at_total = slice(LANES - 3 * HALO - 1, LANES - 3 * HALO)
    upstream = jnp.sum(jnp.where(place < reach, held, 0.0), axis=0)[:, at_total]
    through = jnp.sum(jnp.where(place <= reach, held, 0.0), axis=0)[:, at_total]
    previous = edge_ref[jnp.maximum(reach - 1, 0)]
    following = edge_ref[jnp.minimum(reach + 1, REACHES - 1)]
    none = jnp.zeros((SCENS, LANES), jnp.float32)
    is_left = lane >= LANES // 2

    def outer(row, at, beyond, base, edge, upto):
        resist = jnp.where(beyond, edge, aux_ref[at : at + 1, :])
        running = jnp.where(beyond, base + upto, upstream + aux_ref[24 + at : 25 + at, :])
        return taken(row), taken(row + 1), resist, running

    before = jnp.where(is_high[0:1], 0.0, last_of(previous, 3))
    left = outer(LEFT_ROW, BLOCKS + 1, scen == 0, upstream, last_of(previous, 2), before)
    right = outer(
        RIGHT_ROW, BLOCKS, scen == SCENS - 1, through, first_of(following, 2), first_of(following, 3)
    )
    for j in range(WIDE):
        if j == 0:
            head, flow, resist, running = (jnp.where(is_left, a, b) for a, b in zip(left, right))
        else:
            head, flow = taken(2 * (j - 1)), taken(2 * (j - 1) + 1)
            resist = aux_ref[j - 1 : j, :]
            running = upstream + aux_ref[23 + j : 24 + j, :]
        wide_ref[0, j] = first_head - running * scale + head
        wide_ref[1, j] = mean_flow + flow
        for state in range(4):
            wide_ref[2 + state, j] = none
        wide_ref[6, j] = jnp.broadcast_to(resist, (SCENS, LANES))

    def two_steps(pair, carry):
        for half in range(2):
            plan_rows = pl.ds(pl.multiple_of((2 * pair + half) * SCENS, SCENS), SCENS)
            head_left = plan_ref[0, plan_rows, :]
            small = plan_ref[1, plan_rows, :]
            large = plan_ref[2, plan_rows, :]

            def sent(j):
                head, flow = wide_ref[0, j], wide_ref[1, j]
                friction = wide_ref[6, j] * flow * jnp.abs(flow) + (
                    (wide_ref[2, j] + wide_ref[3, j]) + (wide_ref[4, j] + wide_ref[5, j])
                )
                net = flow - friction
                return pltpu.roll(head + net, 1, 1), pltpu.roll(head - net, LANES - 1, 1)

            ring_start, ring_end = sent(0), sent(WIDE - 1)
            forward_before, (forward, backward) = ring_end[0], ring_start
            for j in range(WIDE):
                forward_after, backward_after = {WIDE - 2: ring_end, WIDE - 1: ring_start}.get(j) or sent(j + 1)
                from_left = jnp.where(is_low, forward_before, forward)
                from_right = jnp.where(is_high, backward_after, backward)
                new_head = 0.5 * (from_left + from_right)
                new_flow = 0.5 * (from_left - from_right)
                if j == 1:
                    new_head = jnp.where(at_first, head_left, new_head)
                    new_flow = jnp.where(at_first, head_left - from_right, new_flow)
                if j == BLOCKS:
                    new_head = jnp.where(at_last, from_left * small, new_head)
                    new_flow = jnp.where(at_last, from_left * large, new_flow)
                change = new_flow - wide_ref[1, j]
                wide_ref[0, j] = new_head
                wide_ref[1, j] = new_flow
                for state in range(4):
                    wide_ref[2 + state, j] = RETAINS[state] * wide_ref[2 + state, j] + SHARES[state] * change
                if 1 <= j <= BLOCKS:
                    for field, value in enumerate((new_head, new_flow)):
                        if half == 0:
                            kept_ref[field, j - 1] = value
                        else:
                            both = jnp.concatenate([kept_ref[field, j - 1], value], axis=0)
                            cols_ref[
                                field,
                                pl.ds(pl.multiple_of(pair * 2 * SCENS, 2 * SCENS), 2 * SCENS),
                                (j - 1) * LANES : j * LANES,
                            ] = both.astype(jnp.bfloat16)
                forward_before, forward, backward = forward, forward_after, backward_after
        return carry

    lax.fori_loop(0, STEPS // 2, two_steps, 0)

    total = None
    for field in range(2):
        columns = cols_ref[field]
        part = lax.dot_general(columns, columns, (((1,), (1,)), ((), ())), preferred_element_type=jnp.float32)
        total = part if total is None else total + part
    order_ref[...] = total
    rows = [order_ref[pl.ds(which, STEPS, stride=SCENS), :] for which in range(SCENS)]
    order_ref[...] = jnp.concatenate(rows, axis=0).T
    rows = [order_ref[pl.ds(which, STEPS, stride=SCENS), :] for which in range(SCENS)]
    quarters = [jnp.concatenate(rows[2 * which : 2 * which + 2], axis=0) for which in range(4)]
    column = lax.broadcasted_iota(jnp.int32, (QUARTER, COLS), 1) // QUARTER
    second = jnp.where(column == 0, pltpu.roll(quarters[2], 2 * QUARTER, 1), quarters[1])
    rest, column = pltpu.roll(rows[7], QUARTER, 1), column[0:STEPS]
    for place, piece in ((1, rows[6]), (2, rows[5]), (3, rows[4])):
        moved = pltpu.roll(piece, (place + 1) * QUARTER, 1) if place < 3 else piece
        rest = jnp.where(column == place, moved, rest)
    packed = jnp.concatenate([quarters[0], second, rest], axis=0)
    for which in range(SCENS):
        for part in range(PIECES):
            at = (which * PIECES + part) * 2
            gram_ref[which, part] = packed[at : at + 2, :]


def fold_kernel(in_ref, out_ref):
    count, copies = in_ref.shape[0], out_ref.shape[0]
    total = in_ref[0]
    for which in range(1, count):
        total = total + in_ref[which]
    for which in range(copies):
        out_ref[which] = total


def basis_kernel(gram_ref, cols_ref, rows_ref, tri_ref, work_ref, turned_ref, order_ref, out_ref, sems):
    scale = 1.0 / (2 * CELLS)
    sub = lax.broadcasted_iota(jnp.int32, (8, COLS), 0)
    lane = lax.broadcasted_iota(jnp.int32, (8, COLS), 1)
    groups = PANEL // 8
    for field in range(2):
        for part in range(SHARE // CHUNK):
            turned_ref[field * (SHARE // CHUNK) + part] = cols_ref[field, :, part * CHUNK : (part + 1) * CHUNK].T
    for which in range(SCENS):
        for part in range(PIECES):
            at = (which * PIECES + part) * 2
            order_ref[at : at + 2, :] = gram_ref[which, part] * scale
    column = lax.broadcasted_iota(jnp.int32, (QUARTER, COLS), 1) // QUARTER
    first, second = order_ref[0:QUARTER, :], order_ref[QUARTER:HALF, :]
    rest = order_ref[HALF : HALF + STEPS, :]
    third = jnp.concatenate([rest, pltpu.roll(rest, QUARTER, 1)], axis=0)
    third = jnp.where(column == 3, third, pltpu.roll(second, 2 * QUARTER, 1))
    fourth = jnp.concatenate([pltpu.roll(rest, 2 * QUARTER, 1), pltpu.roll(rest, 3 * QUARTER, 1)], axis=0)
    mirror = jnp.concatenate([first, second, third, fourth], axis=0).T
    work_ref[0:QUARTER, 0:COLS] = first
    work_ref[QUARTER:HALF, 0:COLS] = jnp.where(column == 0, mirror[QUARTER:HALF, :], second)
    work_ref[HALF : HALF + QUARTER, 0:COLS] = third
    work_ref[HALF + QUARTER :, 0:COLS] = jnp.where(column == 2, mirror[HALF + QUARTER :, :], fourth)
    for g in range(COLS // 8):
        work_ref[8 * g : 8 * g + 8, COLS:] = jnp.where(lane == sub + 8 * g, 1.0, 0.0).astype(jnp.float32)
    inverse_rows = []
    for low in range(0, COLS, PANEL):
        left = [work_ref[low + 8 * g : low + 8 * g + 8, 0:COLS] for g in range(groups)]
        right = [work_ref[low + 8 * g : low + 8 * g + 8, COLS:] for g in range(groups)]
        scaled = []
        for own in range(groups):
            start = low + 8 * own
            wide = {
                g: [jnp.broadcast_to(left[g][:, start + j : start + j + 1], (8, COLS)) for j in range(8)]
                for g in range(own, groups)
            }
            inverses = jnp.zeros((8, COLS), jnp.float32)
            for k in range(8):
                inverse = 1.0 / wide[own][k][k : k + 1, :]
                inverses = jnp.where(sub == k, inverse, inverses)
                ahead = {j: wide[own][j][k : k + 1, :] * inverse for j in range(k + 1, 8)}
                row_left = left[own][k : k + 1, :] * inverse
                row_right = right[own][k : k + 1, :] * inverse
                for g in range(own, groups):
                    factor = wide[g][k]
                    if g == own:
                        factor = jnp.where(sub > k, factor, 0.0)
                    for j in ahead:
                        wide[g][j] = wide[g][j] - factor * ahead[j]
                    left[g] = left[g] - factor * row_left
                    right[g] = right[g] - factor * row_right
            scaled.append(left[own] * inverses)
            root = jnp.sqrt(inverses)
            tri_ref[start : start + 8, :] = jnp.where(lane >= sub + start, left[own] * root, 0.0)
            inverse_rows.append(right[own] * root)
        if low + PANEL < COLS:
            update = lax.dot_general(
                jnp.concatenate(scaled, axis=0),
                jnp.concatenate([jnp.concatenate(left, axis=0), jnp.concatenate(right, axis=0)], axis=1),
                (((0,), (0,)), ((), ())),
                precision=EXACT,
                preferred_element_type=jnp.float32,
            )
            work_ref[low + PANEL :, :] = work_ref[low + PANEL :, :] - update[low + PANEL :, :]
    order_ref[...] = jnp.concatenate(inverse_rows, axis=0).T
    inverse = jnp.concatenate([order_ref[pl.ds(n, SCENS, stride=STEPS), :] for n in range(STEPS)], axis=0)
    high = inverse.astype(jnp.bfloat16)
    rest = inverse - high.astype(jnp.float32)
    middle = rest.astype(jnp.bfloat16)
    both = jnp.concatenate([high, middle], axis=0)
    copies = []
    for field in range(2):
        for part in range(SHARE // CHUNK):
            slot = len(copies)
            piece = turned_ref[slot]
            out_ref[slot] = jnp.dot(
                jnp.concatenate([piece, piece], axis=1), both, preferred_element_type=jnp.float32
            )
            copy = pltpu.make_async_copy(
                out_ref.at[slot], rows_ref.at[field, pl.ds(part * CHUNK, CHUNK), :], sems.at[slot]
            )
            copy.start()
            copies.append(copy)
    for copy in copies:
        copy.wait()


def fold(value, copies):
    return pl.pallas_call(
        fold_kernel,
        out_shape=jax.ShapeDtypeStruct((copies,) + value.shape[1:], jnp.float32),
        compiler_params=params(),
    )(value)


def exchanged(value, axis, groups=None):
    return lax.all_to_all(value, axis, split_axis=0, concat_axis=0, axis_index_groups=groups, tiled=True)


def local(perturb, resist, flow_rate, head_plan, valve_plan):
    f32 = jnp.float32
    vmem = pl.BlockSpec(memory_space=pltpu.VMEM)
    hbm = pl.BlockSpec(memory_space=pltpu.HBM)
    blocks = PART // LANES
    state = perturb.reshape(2, blocks, LANES).transpose(1, 0, 2).reshape(2 * blocks, LANES)
    resist = resist.reshape(LANES, LANES)
    edges = pl.pallas_call(
        edges_kernel,
        in_specs=[hbm, hbm],
        out_specs=vmem,
        out_shape=jax.ShapeDtypeStruct((REACHES, 1, LANES), f32),
        scratch_shapes=[
            pltpu.VMEM((2, 8, LANES), f32),
            pltpu.VMEM((LANES, LANES), f32),
            pltpu.SemaphoreType.DMA((3,)),
        ],
        compiler_params=params(61),
    )(state, resist)
    edges = exchanged(edges, "reach")
    plans = jnp.concatenate([head_plan, valve_plan, flow_rate.reshape(1, 1)], axis=1)
    windows, aux = pl.pallas_call(
        window_kernel,
        in_specs=[vmem, vmem, vmem],
        out_shape=(
            jax.ShapeDtypeStruct((SCENS, WINDOW, LANES), f32),
            jax.ShapeDtypeStruct((48, LANES), f32),
        ),
        compiler_params=params(),
    )(state, resist, plans)
    windows = pl.pallas_call(
        patch_kernel,
        in_specs=[vmem, vmem],
        out_specs=vmem,
        out_shape=jax.ShapeDtypeStruct((SCENS, WINDOW, LANES), f32),
        input_output_aliases={0: 0},
        compiler_params=params(),
    )(windows, edges)
    windows = exchanged(windows, "scen").reshape(SCENS * WINDOW, LANES)
    columns, gram = pl.pallas_call(
        step_kernel,
        out_shape=(
            jax.ShapeDtypeStruct((2, COLS, SHARE), jnp.bfloat16),
            jax.ShapeDtypeStruct((SCENS, PIECES, 2, COLS), f32),
        ),
        scratch_shapes=[
            pltpu.VMEM((7, WIDE, SCENS, LANES), f32),
            pltpu.VMEM((3, STEPS * SCENS, LANES), f32),
            pltpu.VMEM((2, BLOCKS, SCENS, LANES), f32),
            pltpu.VMEM((COLS, COLS), f32),
        ],
        compiler_params=params(),
    )(windows, edges, aux)
    gram = fold(exchanged(gram, "scen"), REACHES)
    gram = fold(exchanged(gram, "reach"), SCENS)
    gram = exchanged(gram, "scen")
    chunks = 2 * SHARE // CHUNK
    return pl.pallas_call(
        basis_kernel,
        in_specs=[vmem, vmem],
        out_specs=(pl.BlockSpec(memory_space=pl.ANY), vmem),
        out_shape=(
            jax.ShapeDtypeStruct((2, SHARE, COLS), f32),
            jax.ShapeDtypeStruct((COLS, COLS), f32),
        ),
        scratch_shapes=[
            pltpu.VMEM((COLS, 2 * COLS), f32),
            pltpu.VMEM((chunks, CHUNK, COLS), jnp.bfloat16),
            pltpu.VMEM((COLS, COLS), f32),
            pltpu.VMEM((chunks, CHUNK, COLS), f32),
            pltpu.SemaphoreType.DMA((chunks,)),
        ],
        compiler_params=params(),
    )(gram, columns)


def solution(mesh):
    in_specs = (P("scen", None, "reach"), P("reach"), P("scen"), P("scen", None), P("scen", None))
    out_specs = (P(None, ("reach", "scen"), None), P())
    return jax.shard_map(local, mesh=mesh, in_specs=in_specs, out_specs=out_specs, check_vma=False)
```
